32 devices in a mesh: hour: 2 (over y), stn: 4 (over x, core), tchunk: 4 (over z).
Axes of the slice: x: 2, y: 2, z: 4, core: 2. Of those that a mesh axis runs over, the one named last changes fastest.
Arguments:
- raw_data: float32 [576, 32768], P('stn', ('hour', 'tchunk')), parts along dimension 1, may hold values from -500 to 500, as said below
- station_group: int32 [576], P('stn'), may hold values from 0 to 15
- partner_blocks: int32 [4, 3], P('stn'), may hold values from -1 to 3, as said below
Outputs:
- cross_spectra: float32 [8, 3, 512, 512], P(('hour', 'stn'), None, 'tchunk'), parts along dimension 0
The draws below stay inside these ranges and needn't reach their ends.
There are 2 independent parts, one for each index of `hour`. The reference program is written for one: setup_inputs(seed, part) draws one part's arguments, and reference() takes and returns one part's arrays. A program takes and returns all parts, laid end to end along the dimension named above; an argument that names none is the same for every part. Nothing has to cross between parts.
Inputs may be any that keep to these rules, and one draw needn't show every extreme that they name: `raw_data`: recorded ground motion. `partner_blocks`: row b holds distinct blocks other than b in its first entries and -1 in the rest; every row has at least one partner and some row has 3.
All inputs are finite; a program needn't handle non-finite values.
Results may differ from the reference program's by a relative error of at most 0.0079.
Values may be sent and summed in bfloat16 or wider, within the bound.
No kernel may reach another device: no remote copies, remote signals or barrier semaphores. Data moves between devices by JAX's collectives and lax.ppermute only.
A program may use at most 128 MiB of HBM per device.

```python
import math
import jax
import jax.numpy as jnp
from jax import lax

STN_DEV = 144
SEGLEN = 4096
HOP = 2048
NBIN = 512
RB = 128
RAMH = 10
SMOOTH = 8
SUB = 16
MAXP = 3
NBLK = 4
STATIONS = 576
SAMPLES = 16384
NSEG = 7


def draw_raw_data(key, part):
    total_blocks = SAMPLES // RB
    station_scale = jnp.exp(jax.random.uniform(jax.random.fold_in(key, 101), (STATIONS, 1, 1), minval=math.log(0.1), maxval=math.log(10.0)))
    envelope = jnp.exp(jax.random.uniform(jax.random.fold_in(key, 102), (STATIONS, total_blocks, 1), minval=0.0, maxval=math.log(10.0)))
    base_motion = jnp.clip(jax.random.normal(jax.random.fold_in(key, 103), (STATIONS, total_blocks, RB)), -4.0, 4.0)
    values = station_scale * envelope * base_motion
    return values.reshape(STATIONS, SAMPLES).astype(jnp.float32)


def draw_partner_blocks(key, part):
    block_rows = jnp.arange(NBLK, dtype=jnp.int32)

    def one_row(block_row):
        shuffle = jax.random.permutation(jax.random.fold_in(key, block_row), NBLK - 1).astype(jnp.int32)
        return (block_row + 1 + shuffle[:MAXP]) % NBLK
    chosen = jax.vmap(one_row)(block_rows)
    partner_count = jax.random.randint(jax.random.fold_in(key, 7001), (NBLK,), 1, MAXP + 1)
    full_row = jax.random.randint(jax.random.fold_in(key, 7002), (), 0, NBLK)
    partner_count = jnp.where(block_rows == full_row, MAXP, partner_count)
    slot_index = jnp.arange(MAXP, dtype=jnp.int32)
    return jnp.where(slot_index[None, :] < partner_count[:, None], chosen, -1).astype(jnp.int32)


def touch_ends(values, stream_key, least, high):
    index_at = [jax.random.randint(jax.random.fold_in(stream_key, axis), (), 0, length) for axis, length in enumerate(values.shape)]
    widest = values.shape.index(max(values.shape))
    neighbour = index_at[:widest] + [(index_at[widest] + 1) % values.shape[widest]] + index_at[widest + 1:]
    return values.at[tuple(index_at)].set(least).at[tuple(neighbour)].set(high)


def setup_inputs(seed: int = 0, part: int = 0) -> dict:
    streams_of = jax.random.split(jax.random.key(seed), 4)
    part_keys = jax.random.split(jax.random.fold_in(streams_of[3], part), 4)
    return {
        "raw_data": draw_raw_data(jax.random.fold_in(jax.random.fold_in(streams_of[3], part), 71), part),
        "station_group": touch_ends(jax.random.randint(streams_of[1], (STATIONS,), 0, SUB), jax.random.fold_in(streams_of[1], 1), 0, SUB - 1).astype(jnp.int32),
        "partner_blocks": draw_partner_blocks(jax.random.fold_in(streams_of[3], 71), part),
    }


EPS_MEAN = 1e-06
LEVEL = 0.05

def dft_table():
    sample = jnp.arange(SEGLEN, dtype=jnp.int32)
    frequency = jnp.arange(1, NBIN + 1, dtype=jnp.int32)
    phases = sample[:, None] * frequency[None, :] % SEGLEN
    angles = phases.astype(jnp.float32) * (2.0 * math.pi / SEGLEN)
    taper_window = 0.5 - 0.5 * jnp.cos(sample.astype(jnp.float32) * (2.0 * math.pi / SEGLEN))
    matrix = jnp.concatenate([taper_window[:, None] * jnp.cos(angles), -taper_window[:, None] * jnp.sin(angles)], axis=1)
    return matrix.astype(jnp.bfloat16)

def smooth_table():
    bin_index = jnp.arange(NBIN, dtype=jnp.int32)
    nearby = (jnp.abs(bin_index[:, None] - bin_index[None, :]) <= SMOOTH).astype(jnp.float32)
    return nearby / lax.optimization_barrier(jnp.sum(nearby, axis=0, keepdims=True))

def whiten(spectra, smoother):
    real_part = spectra[:, :NBIN]
    imag_part = spectra[:, NBIN:]
    powers = real_part * real_part + imag_part * imag_part
    smooth = jnp.dot(powers, smoother, precision=lax.Precision.HIGHEST)
    floor_level = lax.optimization_barrier(jnp.mean(powers, axis=1, keepdims=True)) + 1e-06
    divisor = jnp.sqrt(smooth + LEVEL * floor_level)
    return jnp.concatenate([real_part / divisor, imag_part / divisor], axis=1).astype(jnp.bfloat16)

def cross_terms(mine, others):
    mine = mine.astype(jnp.float32)
    others = others.astype(jnp.float32)
    real_part = mine[:, :, 0]
    imag_part = mine[:, :, 1]
    left_side = jnp.stack([jnp.stack([real_part, imag_part], 2), jnp.stack([imag_part, -real_part], 2)], 0)
    product = jnp.einsum('oqsck,mrsck->mkoqr', left_side, others, precision=lax.Precision.HIGHEST)
    return product.reshape(product.shape[0], product.shape[1], -1)

def reference(raw_data, station_group, partner_blocks):
    total_blocks = SAMPLES // RB
    pieces = raw_data.reshape(STATIONS, total_blocks, RB)
    block_sums = lax.optimization_barrier(jnp.sum(jnp.abs(pieces), axis=2))
    padded = jnp.pad(block_sums, ((0, 0), (RAMH, RAMH)))
    window = padded[:, 0:total_blocks]
    for offset in range(1, 2 * RAMH):
        window = window + padded[:, offset:offset + total_blocks]
    global_block = jnp.arange(total_blocks, dtype=jnp.int32)
    counted = (jnp.minimum(global_block + RAMH, total_blocks) - jnp.maximum(global_block - RAMH, 0)).astype(jnp.float32)
    running = window / (RB * counted)
    normalized = (pieces / (running[:, :, None] + EPS_MEAN)).reshape(STATIONS, SAMPLES).astype(jnp.bfloat16)
    station_hops = normalized.reshape(STATIONS, SAMPLES // HOP, HOP)
    matrix = dft_table()
    smoother = smooth_table()

    def per_block(block_index):
        hops_here = lax.dynamic_slice_in_dim(station_hops, block_index * STN_DEV, STN_DEV, 0)
        group_row = lax.dynamic_slice_in_dim(station_group, block_index * STN_DEV, STN_DEV, 0)
        segments = jnp.concatenate([hops_here[:, :-1], hops_here[:, 1:]], axis=2).reshape(STN_DEV * NSEG, SEGLEN)
        spectra = jnp.dot(segments, matrix, preferred_element_type=jnp.float32)
        whitened = whiten(spectra, smoother)
        member = (group_row[None, :] == jnp.arange(SUB, dtype=jnp.int32)[:, None]).astype(jnp.bfloat16)
        beam_sums = jnp.dot(member, whitened.reshape(STN_DEV, NSEG * 2 * NBIN), preferred_element_type=jnp.float32)
        return beam_sums.astype(jnp.bfloat16).reshape(SUB, NSEG, 2, NBIN)
    beams = lax.map(per_block, jnp.arange(NBLK, dtype=jnp.int32))

    def per_pair(block_index):
        partner_row = partner_blocks[block_index]
        others = beams[jnp.clip(partner_row, 0, NBLK - 1)]
        stacked = cross_terms(beams[block_index], others)
        stacked = jnp.where(partner_row[:, None, None] >= 0, stacked, jnp.float32(0.0))
        return stacked / NSEG
    return lax.map(per_pair, jnp.arange(NBLK, dtype=jnp.int32))
```

```python
import functools
import math

import jax
import jax.numpy as jnp
import ml_dtypes
import numpy as np
from jax import lax
from jax.experimental import pallas as pl
from jax.experimental.pallas import tpu as pltpu
from jax.sharding import PartitionSpec as P

SEG_DEV = 2
SEGLEN = 4096
HOP = 2048
NBIN = 512
RB = 128
RAMH = 10
SMOOTH = 8
SUB = 16
MAXP = 3

EPS_MEAN = 1e-06
LEVEL = 0.05

BF16 = jnp.bfloat16
F32 = jnp.float32
VMEM = pl.BlockSpec(memory_space=pltpu.VMEM)
SMEM = pl.BlockSpec(memory_space=pltpu.SMEM)
MIB = 1 << 20


def dft_table():
    sample = np.arange(SEGLEN, dtype=np.int32)
    frequency = np.arange(1, NBIN + 1, dtype=np.int32)
    phases = sample[:, None] * frequency[None, :] % SEGLEN
    turn = np.arange(SEGLEN, dtype=np.float64) * (2.0 * math.pi / SEGLEN)
    taper = (0.5 - 0.5 * np.cos(turn))[:, None]
    matrix = np.concatenate([taper * np.cos(turn)[phases], -taper * np.sin(turn)[phases]], axis=1)
    return matrix.astype(np.float32).astype(ml_dtypes.bfloat16)


def smooth_tables():
    bin_index = np.arange(NBIN)
    nearby = np.abs(bin_index[:, None] - bin_index[None, :]) <= SMOOTH
    scale = 1.0 / np.sum(nearby, axis=0, keepdims=True)
    return nearby.astype(ml_dtypes.bfloat16), scale.astype(np.float32)


def neighbour_swap(first, second, axis):
    count = lax.axis_size(axis)
    out = []
    for block, start in ((first, 0), (second, 1)):
        pairs = [(i, i + 1) for i in range(start, count - 1, 2)]
        out.append(lax.ppermute(block, axis, pairs + [(j, i) for i, j in pairs]))
    return out


def swapped(block, axis, mask):
    return lax.ppermute(block, axis, [(i, i ^ mask) for i in range(lax.axis_size(axis))])


def call(kernel, out_shape, operands, specs=None, flops=0, limit=16, **more):
    moved = sum(math.prod(a.shape) * a.dtype.itemsize for a in list(operands) + jax.tree.leaves(out_shape))
    more.setdefault("out_specs", jax.tree.map(lambda _: VMEM, out_shape))
    return pl.pallas_call(
        kernel,
        out_shape=out_shape,
        in_specs=specs or [VMEM] * len(operands),
        compiler_params=pltpu.CompilerParams(vmem_limit_bytes=limit * MIB),
        cost_estimate=pl.CostEstimate(flops=flops, bytes_accessed=moved, transcendentals=0),
        **more,
    )(*operands)


def sums_kernel(steps, place, raw, sums, to_even, to_odd, held):
    step = pl.program_id(0)
    rows, samples = raw.shape
    lane = lax.broadcasted_iota(jnp.int32, (rows, RB), 1)
    total = jnp.zeros((rows, RB), F32)
    for b in range(samples // RB):
        here = jnp.sum(jnp.abs(raw[:, b * RB : (b + 1) * RB]), axis=1, keepdims=True)
        total = jnp.where(lane == b, here, total)
    held[pl.ds(step * rows, rows), :] = total

    @pl.when(step == steps - 1)
    def _():
        blocks = samples // RB
        whole = held[...]
        sums[...] = whole[:, :blocks]
        flipped = jnp.transpose(whole)
        head = flipped[: blocks // 2]
        tail = flipped[blocks // 2 : blocks]
        even = place[0] % 2 == 0
        to_even[...] = jnp.where(even, tail, head)
        to_odd[...] = jnp.where(even, head, tail)


def exact_dot(left, right, dims):
    return lax.dot_general(left, right, (dims, ((), ())), precision=lax.Precision.HIGHEST, preferred_element_type=F32)


def normalize_kernel(
    slabs, place, raw, sums, from_even, from_odd, table, normal, to_even, to_odd, keep_right, keep_left
):
    stations, blocks = sums.shape
    half_blocks = from_even.shape[0]
    even = place[0] % 2 == 0
    left = jnp.where(even, from_odd[...], from_even[...])
    right = jnp.where(even, from_even[...], from_odd[...])

    def band(rows, first):
        source = lax.broadcasted_iota(jnp.int32, (rows, blocks), 0) + first
        target = lax.broadcasted_iota(jnp.int32, (rows, blocks), 1)
        return ((source >= target - RAMH) & (source < target + RAMH)).astype(F32)

    window = exact_dot(sums[...], band(blocks, 0), ((1,), (0,)))
    window += exact_dot(left, band(half_blocks, -half_blocks), ((0,), (0,)))
    window += exact_dot(right, band(half_blocks, blocks), ((0,), (0,)))
    block = lax.broadcasted_iota(jnp.int32, (stations, blocks), 1) + place[0] * blocks
    counted = jnp.minimum(block + RAMH, slabs * blocks) - jnp.maximum(block - RAMH, 0)
    factor = 1.0 / (window / (RB * counted.astype(F32)) + EPS_MEAN)
    for b in range(blocks):
        here = pl.ds(b * RB, RB)
        normal[:, here] = (raw[:, here] * factor[:, b : b + 1]).astype(BF16)

    half = stations // 2

    def crossing(first, second):
        return jnp.dot(normal[:, first : first + HOP], table[second : second + HOP, :], preferred_element_type=F32)

    ahead = crossing(HOP, 0)
    keep_right[...] = ahead[:half]
    for_right = ahead[half:].astype(BF16)
    behind = crossing(0, HOP)
    keep_left[...] = behind[half:]
    for_left = behind[:half].astype(BF16)

    @pl.when(even)
    def _():
        to_even[...] = for_right
        to_odd[...] = for_left

    @pl.when(jnp.logical_not(even))
    def _():
        to_even[...] = for_left
        to_odd[...] = for_right


def whiten(spectra, nearby, scale):
    real_part = spectra[:, :NBIN]
    imag_part = spectra[:, NBIN:]
    powers = real_part * real_part + imag_part * imag_part
    high = powers.astype(BF16)
    low = (powers - high.astype(F32)).astype(BF16)
    smooth = jnp.dot(high, nearby, preferred_element_type=F32) + jnp.dot(low, nearby, preferred_element_type=F32)
    floor_level = jnp.sum(powers, axis=1, keepdims=True) * (1.0 / NBIN) + 1e-06
    inverse = lax.rsqrt(smooth * scale + LEVEL * floor_level)
    return (real_part * inverse).astype(BF16), (imag_part * inverse).astype(BF16)


def members(group, count):
    shape = (count, group.shape[1])
    return (lax.broadcasted_iota(jnp.int32, shape, 0) == group).astype(BF16)


def own_kernel(normal, table, group, nearby, scale, beams):
    spectra = jnp.dot(normal[...], table[...], preferred_element_type=F32)
    member = members(group[...], SUB)
    for part, white in enumerate(whiten(spectra, nearby[...], scale[...])):
        beams[part * SUB : (part + 1) * SUB, :] = jnp.dot(member, white, preferred_element_type=F32).astype(BF16)


def crossing_kernel(place, keep_right, keep_left, from_even, from_odd, own, group, nearby, scale, *out):
    half = keep_right.shape[0]
    held = out[-1]
    even = place[0] % 2 == 0
    got_even = from_even[...].astype(F32)
    got_odd = from_odd[...].astype(F32)
    ahead = keep_right[...] + jnp.where(even, got_even, got_odd)
    behind = keep_left[...] + jnp.where(even, got_odd, got_even)
    spectra = jnp.concatenate([ahead, behind], axis=0)
    station = lax.broadcasted_iota(jnp.int32, group.shape, 1)
    member = members(group[...] + jnp.where(station < half, 0, SUB), 2 * SUB)
    held[: 2 * SUB, :] = own[...]
    for part, white in enumerate(whiten(spectra, nearby[...], scale[...])):
        sums = jnp.dot(member, white, preferred_element_type=F32).astype(BF16)
        for side in range(2):
            row = (2 + 2 * side + part) * SUB
            held[row : row + SUB, :] = sums[side * SUB : (side + 1) * SUB]
    pieces = len(out) - 1
    if pieces > 1:
        width = NBIN // pieces
        for mask in range(pieces):
            start = pl.multiple_of((place[0] ^ mask) * width, width)
            out[mask][...] = held[:, pl.ds(start, width)]
    else:
        out[0][...] = held[...]


def cross_kernel(segments, place, partners, *refs):
    blocks, out, mine, others = refs[:-3], refs[-3], refs[-2], refs[-1]
    slot = pl.program_id(0)
    width = out.shape[1]
    lane = lax.broadcasted_iota(jnp.int32, (SUB, SUB * SUB), 1)
    row = lax.broadcasted_iota(jnp.int32, (SUB, SUB * SUB), 0)
    spread = (lane // SUB == row).astype(BF16)
    tiled = (lane % SUB == row).astype(BF16)
    count = (segments + 1) // 2

    def grown(piece, pattern):
        return lax.dot_general(piece, pattern, (((0,), (0,)), ((), ())), preferred_element_type=F32)

    def segment(block, s, part):
        source = block.at[s // 2]
        if s % 2 == 0:
            return source[part * SUB : (part + 1) * SUB, :]
        ahead = source[(2 + part) * SUB : (3 + part) * SUB, :].astype(F32)
        behind = block[s // 2 + 1, (4 + part) * SUB : (5 + part) * SUB, :].astype(F32)
        return (ahead + behind).astype(BF16)

    partner = partners[0, slot]

    @pl.when(slot == 0)
    def _():
        own = blocks[0]
        for s in range(segments):
            for part in range(2):
                mine[s, part] = grown(segment(own, s, part), spread)

    @pl.when(partner < 0)
    def _():
        out[...] = jnp.zeros_like(out)

    @pl.when(partner >= 0)
    def _():
        which = partner ^ place[1]
        for index in range(1, len(blocks)):
            @pl.when(which == index)
            def _(index=index):
                others[...] = blocks[index][...]
        real_sum = jnp.zeros((width, SUB * SUB), F32)
        imag_sum = jnp.zeros((width, SUB * SUB), F32)
        for s in range(segments):
            a, b = mine[s, 0], mine[s, 1]
            c, d = grown(segment(others, s, 0), tiled), grown(segment(others, s, 1), tiled)
            real_sum += a * c + b * d
            imag_sum += b * c - a * d
        out[0, :, : SUB * SUB] = real_sum * (1.0 / segments)
        out[0, :, SUB * SUB :] = imag_sum * (1.0 / segments)


def body(raw_data, station_group, partner_blocks):
    stations, samples = raw_data.shape
    slabs = lax.axis_size("tchunk")
    count_blocks = lax.axis_size("stn")
    me = lax.axis_index("tchunk")
    place = jnp.stack([me, lax.axis_index("stn")]).astype(jnp.int32)
    blocks = samples // RB
    half = stations // 2
    table = jnp.asarray(dft_table())
    nearby, scale = (jnp.asarray(t) for t in smooth_tables())
    group = station_group[None, :]
    shape = jax.ShapeDtypeStruct

    steps = 3
    halo = shape((blocks // 2, stations), F32)
    sums, even, odd = call(
        functools.partial(sums_kernel, steps),
        (shape((stations, blocks), F32), halo, halo),
        (place, raw_data),
        specs=[SMEM, pl.BlockSpec((stations // steps, samples), lambda i: (i, 0))],
        out_specs=[pl.BlockSpec((stations, blocks), lambda i: (0, 0))]
        + [pl.BlockSpec(halo.shape, lambda i: (0, 0))] * 2,
        grid=(steps,),
        scratch_shapes=[pltpu.VMEM((stations, RB), F32)],
        flops=2 * stations * samples,
    )
    even, odd = neighbour_swap(even, odd, "tchunk")
    sent = shape((half, 2 * NBIN), BF16)
    kept = shape((half, 2 * NBIN), F32)
    normal, even, odd, keep_right, keep_left = call(
        functools.partial(normalize_kernel, slabs),
        (shape((stations, samples), BF16), sent, sent, kept, kept),
        (place, raw_data, sums, even, odd, table),
        specs=[SMEM] + [VMEM] * 5,
        flops=4 * stations * samples * NBIN,
        limit=32,
    )
    even, odd = neighbour_swap(even, odd, "tchunk")
    own = call(
        own_kernel,
        shape((2 * SUB, NBIN), BF16),
        (normal, table, group, nearby, scale),
        flops=4 * stations * samples * NBIN,
        limit=32,
    )
    direct = slabs <= 8 and slabs & (slabs - 1) == 0 and NBIN // slabs % 128 == 0
    width = NBIN // slabs
    rows = 6 * SUB
    pieces = call(
        crossing_kernel,
        tuple([shape((rows, width), BF16)] * slabs) if direct else (shape((rows, NBIN), BF16),),
        (place, keep_right, keep_left, even, odd, own, group, nearby, scale),
        specs=[SMEM] + [VMEM] * 8,
        scratch_shapes=[pltpu.VMEM((rows, NBIN), BF16)],
        flops=8 * stations * NBIN * NBIN,
        limit=32,
    )
    if direct:
        received = [pieces[0]] + [swapped(pieces[m], "tchunk", m) for m in range(1, slabs)]
        order = jnp.arange(slabs) ^ me
        mine = jnp.stack(received, 0)[order]
    else:
        mine = jnp.moveaxis(pieces[0].reshape(rows, slabs, width), 1, 0)
        mine = lax.all_to_all(mine, "tchunk", split_axis=0, concat_axis=0, tiled=True)
    segments = SEG_DEV * slabs - 1
    if count_blocks <= 4 and count_blocks & (count_blocks - 1) == 0:
        others = [mine] + [swapped(mine, "stn", m) for m in range(1, count_blocks)]
    else:
        gathered = lax.all_gather(mine, "stn", axis=0)
        others = [lax.dynamic_index_in_dim(gathered, place[1] ^ m, 0, keepdims=False) for m in range(count_blocks)]
    out = call(
        functools.partial(cross_kernel, segments),
        shape((MAXP, width, 2 * SUB * SUB), F32),
        (place, partner_blocks, *others),
        specs=[SMEM, SMEM] + [VMEM] * count_blocks,
        out_specs=pl.BlockSpec((1, width, 2 * SUB * SUB), lambda i: (i, 0, 0)),
        grid=(MAXP,),
        scratch_shapes=[pltpu.VMEM((segments, 2, width, SUB * SUB), F32), pltpu.VMEM(mine.shape, BF16)],
        flops=MAXP * segments * width * SUB * SUB * 8,
        limit=32,
    )
    return out[None]


def solution(mesh):
    placed = (P("stn", ("hour", "tchunk")), P("stn"), P("stn", None))
    return jax.shard_map(
        body,
        mesh=mesh,
        in_specs=placed,
        out_specs=P(("hour", "stn"), None, "tchunk", None),
        check_vma=False,
    )
```

```python
import functools
import math

import jax
import jax.numpy as jnp
import ml_dtypes
import numpy as np
from jax import lax
from jax.experimental import pallas as pl
from jax.experimental.pallas import tpu as pltpu
from jax.sharding import PartitionSpec as P

SEG_DEV = 2
SEGLEN = 4096
HOP = 2048
NBIN = 512
RB = 128
RAMH = 10
SMOOTH = 8
SUB = 16
MAXP = 3

EPS_MEAN = 1e-06
LEVEL = 0.05

BF16 = jnp.bfloat16
F32 = jnp.float32
VMEM = pl.BlockSpec(memory_space=pltpu.VMEM)
HBM = pl.BlockSpec(memory_space=pltpu.HBM)
SMEM = pl.BlockSpec(memory_space=pltpu.SMEM)
MIB = 1 << 20


def dft_tables():
    sample = np.arange(HOP, dtype=np.int32)
    frequency = np.arange(1, NBIN + 1, dtype=np.int32)
    turn = np.arange(SEGLEN, dtype=np.float64) * (2.0 * math.pi / SEGLEN)
    phases = sample[:, None] * frequency[None, :] % SEGLEN
    matrix = np.concatenate([np.cos(turn)[phases], -np.sin(turn)[phases]], axis=1)
    taper = (0.5 - 0.5 * np.cos(turn)).reshape(2, HOP)
    sign = np.concatenate([(-1.0) ** frequency] * 2)[None, :]
    matrix = matrix.astype(np.float32).astype(ml_dtypes.bfloat16)
    return matrix, taper.astype(np.float32), sign.astype(np.float32)


def smooth_tables():
    bin_index = np.arange(NBIN)
    nearby = np.abs(bin_index[:, None] - bin_index[None, :]) <= SMOOTH
    scale = 1.0 / np.sum(nearby, axis=0, keepdims=True)
    return nearby.astype(ml_dtypes.bfloat16), scale.astype(np.float32)


def neighbour_swap(first, second):
    blocks, slabs = lax.axis_size("stn"), lax.axis_size("tchunk")
    inner = [(i, i ^ 1) for i in range(slabs - slabs % 2)]
    outer = [(i, i + 1) for i in range(1, slabs - 1, 2)]
    outer += [(j, i) for i, j in outer]
    pairs = [[(b * slabs + i, b * slabs + j) for b in range(blocks) for i, j in part] for part in (inner, outer)]
    if blocks % 2 == 0 and slabs % 2 == 0:
        pairs[1] += [(b * slabs + i, (b ^ 1) * slabs + i) for b in range(blocks) for i in (0, slabs - 1)]
    return [lax.ppermute(block, ("stn", "tchunk"), part) for block, part in zip((first, second), pairs)]


def swapped(block, axis, mask):
    return lax.ppermute(block, axis, [(i, i ^ mask) for i in range(lax.axis_size(axis))])


def call(kernel, out_shape, operands, specs=None, flops=0, limit=16, **more):
    moved = sum(math.prod(a.shape) * a.dtype.itemsize for a in list(operands) + jax.tree.leaves(out_shape))
    more.setdefault("out_specs", jax.tree.map(lambda _: VMEM, out_shape))
    return pl.pallas_call(
        kernel,
        out_shape=out_shape,
        in_specs=specs or [VMEM] * len(operands),
        compiler_params=pltpu.CompilerParams(vmem_limit_bytes=limit * MIB),
        cost_estimate=pl.CostEstimate(flops=flops, bytes_accessed=moved, transcendentals=0),
        **more,
    )(*operands)


def sums_kernel(place, source, raw, sums, to_even, to_odd, held, arrived):
    chunks = arrived.shape[0]
    stations, samples = raw.shape
    rows = stations // chunks
    blocks = samples // RB
    copies = []
    for step in range(chunks):
        here = pl.ds(step * rows, rows)
        copies.append(pltpu.make_async_copy(source.at[here], raw.at[here], arrived.at[step]))
        copies[-1].start()
    lane = lax.broadcasted_iota(jnp.int32, (rows, RB), 1)
    for step in range(chunks):
        copies[step].wait()
        here = pl.ds(step * rows, rows)
        total = jnp.zeros((rows, RB), F32)
        for b in range(blocks):
            amount = jnp.sum(jnp.abs(raw[here, b * RB : (b + 1) * RB]), axis=1, keepdims=True)
            total = jnp.where(lane == b, amount, total)
        held[here, :] = total
    whole = held[...]
    sums[...] = whole[:, :blocks]
    flipped = jnp.transpose(whole)
    head = flipped[: blocks // 2]
    tail = flipped[blocks // 2 : blocks]
    even = place[0] % 2 == 0
    to_even[...] = jnp.where(even, tail, head)
    to_odd[...] = jnp.where(even, head, tail)


def exact_dot(left, right, dims):
    return lax.dot_general(left, right, (dims, ((), ())), precision=lax.Precision.HIGHEST, preferred_element_type=F32)


def band(rows, blocks, first):
    source = lax.broadcasted_iota(jnp.int32, (rows, blocks), 0) + first
    target = lax.broadcasted_iota(jnp.int32, (rows, blocks), 1)
    return ((source >= target - RAMH) & (source < target + RAMH)).astype(F32)


def scale_blocks(raw, factor, taper, some, normal, windowed):
    for place, b in enumerate(some):
        here = pl.ds(place * RB, RB)
        scaled = (raw[:, b * RB : (b + 1) * RB] * factor[:, b : b + 1]).astype(BF16)
        normal[:, here] = scaled
        hop, inside = divmod(b * RB, HOP)
        weight = taper[1 - hop : 2 - hop, inside : inside + RB]
        windowed[:, here] = (scaled.astype(F32) * weight).astype(BF16)


def middle_kernel(raw, sums, source, taper, table, normal, ahead, behind, windowed, arrived):
    copy = pltpu.make_async_copy(source, table, arrived)
    copy.start()
    blocks = sums.shape[1]
    window = exact_dot(sums[...], band(blocks, blocks, 0), ((1,), (0,)))
    factor = 1.0 / (window * (1.0 / (2 * RAMH * RB)) + EPS_MEAN)
    scale_blocks(raw, factor, taper, range(RAMH, blocks - RAMH + 1), normal, windowed)
    copy.wait()
    split = HOP - RAMH * RB
    rest = windowed.shape[1] - split
    ahead[...] = jnp.dot(windowed[:, split:], table[:rest, :], preferred_element_type=F32)
    behind[...] = jnp.dot(windowed[:, :split], table[HOP - split :, :], preferred_element_type=F32)


def normalize_kernel(
    slabs, place, raw, sums, from_even, from_odd, table, taper, sign, ahead, behind,
    normal, to_even, to_odd, keep_right, keep_left, windowed,
):
    stations, blocks = sums.shape
    half_blocks = from_even.shape[0]
    even = place[0] % 2 == 0
    left = jnp.where(even, from_odd[...], from_even[...])
    right = jnp.where(even, from_even[...], from_odd[...])
    left = jnp.where(place[0] > 0, left, 0.0)
    right = jnp.where(place[0] < slabs - 1, right, 0.0)
    window = exact_dot(sums[...], band(blocks, blocks, 0), ((1,), (0,)))
    window += exact_dot(left, band(half_blocks, blocks, -half_blocks), ((0,), (0,)))
    window += exact_dot(right, band(half_blocks, blocks, blocks), ((0,), (0,)))
    block = lax.broadcasted_iota(jnp.int32, (stations, blocks), 1) + place[0] * blocks
    counted = jnp.minimum(block + RAMH, slabs * blocks) - jnp.maximum(block - RAMH, 0)
    factor = 1.0 / (window / (RB * counted.astype(F32)) + EPS_MEAN)
    outer = [*range(RAMH), *range(blocks - RAMH + 1, blocks)]
    scale_blocks(raw, factor, taper, outer, normal, windowed)

    half = stations // 2
    width = NBIN // 2
    split = RAMH * RB
    rest = windowed.shape[1] - split

    def keep(to_right, to_left):
        for n in range(table.shape[1] // width):
            here = pl.ds(n * width, width)
            right_part = jnp.dot(windowed[:, split:], table[HOP - rest :, here], preferred_element_type=F32)
            right_part += ahead[:, here]
            keep_right[:, here] = right_part[:half]
            to_right[:, here] = right_part[half:].astype(BF16)
            left_part = jnp.dot(windowed[:, :split], table[:split, here], preferred_element_type=F32)
            left_part = (left_part + behind[:, here]) * sign[:, here]
            keep_left[:, here] = left_part[half:]
            to_left[:, here] = left_part[:half].astype(BF16)

    @pl.when(even)
    def _():
        keep(to_even, to_odd)

    @pl.when(jnp.logical_not(even))
    def _():
        keep(to_odd, to_even)


def whiten(spectra, nearby, scale):
    real_part = spectra[:, :NBIN]
    imag_part = spectra[:, NBIN:]
    powers = real_part * real_part + imag_part * imag_part
    high = powers.astype(BF16)
    low = (powers - high.astype(F32)).astype(BF16)
    smooth = jnp.dot(high, nearby, preferred_element_type=F32) + jnp.dot(low, nearby, preferred_element_type=F32)
    floor_level = jnp.sum(powers, axis=1, keepdims=True) * (1.0 / NBIN) + 1e-06
    inverse = lax.rsqrt(smooth * scale + LEVEL * floor_level)
    return (real_part * inverse).astype(BF16), (imag_part * inverse).astype(BF16)


def members(group, count):
    shape = (count, group.shape[1])
    return (lax.broadcasted_iota(jnp.int32, shape, 0) == group).astype(BF16)


def own_kernel(outer, middle, table, taper, sign, group, nearby, scale, beams, windowed):
    stations = outer.shape[0]
    first = RAMH * RB
    last = first + middle.shape[1]
    parts = ((outer, 0, 0, first), (middle, 0, first, HOP), (middle, HOP - first, HOP, last), (outer, first, last, 2 * HOP))
    for source, start, low, high in parts:
        hop, inside = divmod(low, HOP)
        here = source[:, start : start + high - low].astype(F32) * taper[hop : hop + 1, inside : inside + high - low]
        windowed[hop * stations : (hop + 1) * stations, inside : inside + high - low] = here.astype(BF16)
    both = jnp.dot(windowed[...], table[...], preferred_element_type=F32)
    spectra = both[:stations] + both[stations:] * sign[...]
    member = members(group[...], SUB)
    for part, white in enumerate(whiten(spectra, nearby[...], scale[...])):
        beams[part * SUB : (part + 1) * SUB, :] = jnp.dot(member, white, preferred_element_type=F32).astype(BF16)


def crossing_kernel(place, keep_right, keep_left, from_even, from_odd, own, group, nearby, scale, *out):
    half = keep_right.shape[0]
    held = out[-1]
    even = place[0] % 2 == 0
    got_even = from_even[...].astype(F32)
    got_odd = from_odd[...].astype(F32)
    ahead = keep_right[...] + jnp.where(even, got_even, got_odd)
    behind = keep_left[...] + jnp.where(even, got_odd, got_even)
    spectra = jnp.concatenate([ahead, behind], axis=0)
    station = lax.broadcasted_iota(jnp.int32, group.shape, 1)
    member = members(group[...] + jnp.where(station < half, 0, SUB), 2 * SUB)
    held[: 2 * SUB, :] = own[...]
    for part, white in enumerate(whiten(spectra, nearby[...], scale[...])):
        sums = jnp.dot(member, white, preferred_element_type=F32).astype(BF16)
        for side in range(2):
            row = (2 + 2 * side + part) * SUB
            held[row : row + SUB, :] = sums[side * SUB : (side + 1) * SUB]
    pieces = len(out) - 1
    if pieces > 1:
        width = NBIN // pieces
        for mask in range(pieces):
            start = pl.multiple_of((place[0] ^ mask) * width, width)
            out[mask][...] = held[:, pl.ds(start, width)]
    else:
        out[0][...] = held[...]


def cross_kernel(segments, slabs, place, partners, *refs):
    blocks, (out, mine, others, held) = refs[:-4], refs[-4:]
    slot = pl.program_id(0)
    width = out.shape[1]
    partner = partners[0, slot]

    def pick(target, block):
        for m in range(slabs):
            held[place[0] ^ m] = block[m * 6 * SUB : (m + 1) * 6 * SUB, :]
        for s in range(segments):
            source = held.at[s // 2]
            for part in range(2):
                if s % 2 == 0:
                    target[s, part] = source[part * SUB : (part + 1) * SUB, :].astype(F32)
                else:
                    ahead = source[(2 + part) * SUB : (3 + part) * SUB, :].astype(F32)
                    behind = held[s // 2 + 1, (4 + part) * SUB : (5 + part) * SUB, :].astype(F32)
                    target[s, part] = (ahead + behind).astype(BF16).astype(F32)

    @pl.when(slot == 0)
    def _():
        pick(mine, blocks[0])

    @pl.when(partner < 0)
    def _():
        out[...] = jnp.zeros_like(out)

    @pl.when(partner >= 0)
    def _():
        which = partner ^ place[1]
        for index in range(1, len(blocks)):
            @pl.when(which == index)
            def _(index=index):
                pick(others, blocks[index])
        real, imag = [], []
        for q in range(SUB):
            real_sum = jnp.zeros((SUB, width), F32)
            imag_sum = jnp.zeros((SUB, width), F32)
            for s in range(segments):
                a, b = mine[s, 0, q : q + 1, :], mine[s, 1, q : q + 1, :]
                c, d = others[s, 0], others[s, 1]
                real_sum += a * c + b * d
                imag_sum += b * c - a * d
            real.append(real_sum * (1.0 / segments))
            imag.append(imag_sum * (1.0 / segments))
        half = SUB * SUB
        out[0, :, :half] = jnp.transpose(jnp.concatenate(real, axis=0))
        out[0, :, half:] = jnp.transpose(jnp.concatenate(imag, axis=0))


def body(raw_data, station_group, partner_blocks):
    stations, samples = raw_data.shape
    slabs = lax.axis_size("tchunk")
    count_blocks = lax.axis_size("stn")
    me = lax.axis_index("tchunk")
    place = jnp.stack([me, lax.axis_index("stn")]).astype(jnp.int32)
    blocks = samples // RB
    half = stations // 2
    table, taper, sign = (jnp.asarray(t) for t in dft_tables())
    nearby, scale = (jnp.asarray(t) for t in smooth_tables())
    group = station_group[None, :]
    shape = jax.ShapeDtypeStruct

    halo = shape((blocks // 2, stations), F32)
    in_hbm = [pltpu.with_memory_space_constraint(a, pltpu.HBM) for a in (raw_data, table)]
    raw, sums, even, odd = call(
        sums_kernel,
        (shape(raw_data.shape, F32), shape((stations, blocks), F32), halo, halo),
        (place, in_hbm[0]),
        specs=[SMEM, HBM],
        scratch_shapes=[pltpu.VMEM((stations, RB), F32), pltpu.SemaphoreType.DMA((6,))],
        flops=2 * stations * samples,
    )
    even, odd = neighbour_swap(even, odd)
    sent = shape((half, 2 * NBIN), BF16)
    kept = shape((half, 2 * NBIN), F32)
    inner = (blocks - 2 * RAMH + 1) * RB
    partial = shape((stations, 2 * NBIN), F32)
    table, middle, ahead, behind = call(
        middle_kernel,
        (shape(table.shape, BF16), shape((stations, inner), BF16), partial, partial),
        (raw, sums, in_hbm[1], taper),
        specs=[VMEM, VMEM, HBM, VMEM],
        scratch_shapes=[pltpu.VMEM((stations, inner), BF16), pltpu.SemaphoreType.DMA],
        flops=4 * stations * inner * NBIN,
    )
    edge = shape((stations, samples - inner), BF16)
    outer, even, odd, keep_right, keep_left = call(
        functools.partial(normalize_kernel, slabs),
        (edge, sent, sent, kept, kept),
        (place, raw, sums, even, odd, table, taper, sign, ahead, behind),
        specs=[SMEM] + [VMEM] * 9,
        scratch_shapes=[pltpu.VMEM(edge.shape, BF16)],
        flops=4 * stations * samples * NBIN,
        limit=16,
    )
    even, odd = neighbour_swap(even, odd)
    own = call(
        own_kernel,
        shape((2 * SUB, NBIN), BF16),
        (outer, middle, table, taper, sign, group, nearby, scale),
        scratch_shapes=[pltpu.VMEM((2 * stations, HOP), BF16)],
        flops=4 * stations * samples * NBIN,
        limit=32,
    )
    direct = slabs <= 8 and slabs & (slabs - 1) == 0 and NBIN // slabs % 128 == 0
    width = NBIN // slabs
    rows = 6 * SUB
    pieces = call(
        crossing_kernel,
        tuple([shape((rows, width), BF16)] * slabs) if direct else (shape((rows, NBIN), BF16),),
        (place, keep_right, keep_left, even, odd, own, group, nearby, scale),
        specs=[SMEM] + [VMEM] * 8,
        scratch_shapes=[pltpu.VMEM((rows, NBIN), BF16)],
        flops=8 * stations * NBIN * NBIN,
        limit=32,
    )
    if direct:
        order = sorted(range(1, slabs), key=lambda m: (m % 2 == 0, m))
        received = {m: swapped(pieces[m], "tchunk", m) for m in order}
        mine = jnp.concatenate([pieces[0]] + [received[m] for m in range(1, slabs)], axis=0)
    else:
        mine = pieces[0].reshape(rows, slabs, width).swapaxes(0, 1)
        mine = lax.all_to_all(mine, "tchunk", split_axis=0, concat_axis=0, tiled=True)
        mine = mine[jnp.arange(slabs) ^ me].reshape(slabs * rows, width)
    segments = SEG_DEV * slabs - 1
    if count_blocks == 4:
        across = swapped(mine, "stn", 2)
        others = [mine, swapped(mine, "stn", 1), across, swapped(across, "stn", 1)]
    else:
        gathered = lax.all_gather(mine, "stn", axis=0)
        others = [lax.dynamic_index_in_dim(gathered, place[1] ^ m, 0, keepdims=False) for m in range(count_blocks)]
    out = call(
        functools.partial(cross_kernel, segments, slabs),
        shape((MAXP, width, 2 * SUB * SUB), F32),
        (place, partner_blocks, *others),
        specs=[SMEM, SMEM] + [VMEM] * count_blocks,
        out_specs=pl.BlockSpec((1, width, 2 * SUB * SUB), lambda i: (i, 0, 0)),
        grid=(MAXP,),
        scratch_shapes=[pltpu.VMEM((segments, 2, SUB, width), F32)] * 2 + [pltpu.VMEM((slabs, rows, width), BF16)],
        flops=MAXP * segments * width * SUB * SUB * 8,
        limit=32,
    )
    return out[None]


def solution(mesh):
    placed = (P("stn", ("hour", "tchunk")), P("stn"), P("stn", None))
    return jax.shard_map(
        body,
        mesh=mesh,
        in_specs=placed,
        out_specs=P(("hour", "stn"), None, "tchunk", None),
        check_vma=False,
    )
```

```python
import functools
import math

import jax
import jax.numpy as jnp
import ml_dtypes
import numpy as np
from jax import lax
from jax.experimental import pallas as pl
from jax.experimental.pallas import tpu as pltpu
from jax.sharding import PartitionSpec as P

SEG_DEV = 2
SEGLEN = 4096
HOP = 2048
NBIN = 512
RB = 128
RAMH = 10
SMOOTH = 8
SUB = 16
MAXP = 3

EPS_MEAN = 1e-06
LEVEL = 0.05

BF16 = jnp.bfloat16
F32 = jnp.float32
VMEM = pl.BlockSpec(memory_space=pltpu.VMEM)
HBM = pl.BlockSpec(memory_space=pltpu.HBM)
MIB = 1 << 20


def dft_tables():
    sample = np.arange(HOP, dtype=np.int32)
    frequency = np.arange(1, NBIN + 1, dtype=np.int32)
    turn = np.arange(SEGLEN, dtype=np.float64) * (2.0 * math.pi / SEGLEN)
    phases = sample[:, None] * frequency[None, :] % SEGLEN
    matrix = np.concatenate([np.cos(turn)[phases], -np.sin(turn)[phases]], axis=1)
    taper = (0.5 - 0.5 * np.cos(turn)).reshape(2, HOP)
    matrix = matrix.astype(np.float32).astype(ml_dtypes.bfloat16)
    return matrix, taper.astype(np.float32)


def smooth_tables():
    bin_index = np.arange(NBIN)
    nearby = np.abs(bin_index[:, None] - bin_index[None, :]) <= SMOOTH
    scale = 1.0 / np.sum(nearby, axis=0, keepdims=True)
    return nearby.astype(ml_dtypes.bfloat16), scale.astype(np.float32)


def neighbour_swap(first, second):
    blocks, slabs = lax.axis_size("stn"), lax.axis_size("tchunk")
    inner = [(i, i ^ 1) for i in range(slabs - slabs % 2)]
    outer = [(i, i + 1) for i in range(1, slabs - 1, 2)]
    outer += [(j, i) for i, j in outer]
    pairs = [[(b * slabs + i, b * slabs + j) for b in range(blocks) for i, j in part] for part in (inner, outer)]
    if blocks % 2 == 0 and slabs % 2 == 0:
        pairs[1] += [(b * slabs + i, (b ^ 1) * slabs + i) for b in range(blocks) for i in (0, slabs - 1)]
    return [lax.ppermute(block, ("stn", "tchunk"), part) for block, part in zip((first, second), pairs)]


def swapped(block, axis, mask):
    return lax.ppermute(block, axis, [(i, i ^ mask) for i in range(lax.axis_size(axis))])


def call(kernel, out_shape, operands, specs=None, flops=0, limit=16, **more):
    moved = sum(math.prod(a.shape) * a.dtype.itemsize for a in list(operands) + jax.tree.leaves(out_shape))
    more.setdefault("out_specs", jax.tree.map(lambda _: VMEM, out_shape))
    return pl.pallas_call(
        kernel,
        out_shape=out_shape,
        in_specs=specs or [VMEM] * len(operands),
        compiler_params=pltpu.CompilerParams(vmem_limit_bytes=limit * MIB),
        cost_estimate=pl.CostEstimate(flops=flops, bytes_accessed=moved, transcendentals=0),
        **more,
    )(*operands)


def sums_kernel(source, taper_source, raw, sums, to_even, to_odd, taper, held, arrived):
    chunks = arrived.shape[0] - 1
    stations, samples = raw.shape
    rows = stations // chunks
    blocks = samples // RB
    copies = []
    for step in range(chunks):
        here = pl.ds(step * rows, rows)
        copies.append(pltpu.make_async_copy(source.at[here], raw.at[here], arrived.at[step]))
        copies[-1].start()
    copies.append(pltpu.make_async_copy(taper_source, taper, arrived.at[chunks]))
    copies[-1].start()
    lane = lax.broadcasted_iota(jnp.int32, (rows, RB), 1)
    for step in range(chunks):
        copies[step].wait()
        here = pl.ds(step * rows, rows)
        total = jnp.zeros((rows, RB), F32)
        for b in range(blocks):
            amount = jnp.sum(jnp.abs(raw[here, b * RB : (b + 1) * RB]), axis=1, keepdims=True)
            total = jnp.where(lane == b, amount, total)
        held[here, :] = total
    whole = held[...]
    sums[...] = whole[:, :blocks]
    flipped = jnp.transpose(whole)
    head = flipped[: blocks // 2]
    tail = flipped[blocks // 2 : blocks]
    even = lax.axis_index("tchunk") % 2 == 0
    to_even[...] = jnp.where(even, tail, head)
    to_odd[...] = jnp.where(even, head, tail)
    copies[-1].wait()


def exact_dot(left, right, dims):
    return lax.dot_general(left, right, (dims, ((), ())), precision=lax.Precision.HIGHEST, preferred_element_type=F32)


def band(rows, blocks, first):
    source = lax.broadcasted_iota(jnp.int32, (rows, blocks), 0) + first
    target = lax.broadcasted_iota(jnp.int32, (rows, blocks), 1)
    return ((source >= target - RAMH) & (source < target + RAMH)).astype(F32)


def alternating():
    column = lax.broadcasted_iota(jnp.int32, (1, 2 * NBIN), 1)
    return jnp.where(column % 2 == 0, -1.0, 1.0)


def scale_blocks(raw, factor, taper, some, normal, windowed):
    for place, b in enumerate(some):
        here = pl.ds(place * RB, RB)
        scaled = (raw[:, b * RB : (b + 1) * RB] * factor[:, b : b + 1]).astype(BF16)
        normal[:, here] = scaled
        hop, inside = divmod(b * RB, HOP)
        weight = taper[1 - hop : 2 - hop, inside : inside + RB]
        windowed[:, here] = (scaled.astype(F32) * weight).astype(BF16)


def middle_kernel(raw, sums, source, taper, table, normal, ahead, behind, windowed, arrived):
    copy = pltpu.make_async_copy(source, table, arrived)
    copy.start()
    blocks = sums.shape[1]
    window = exact_dot(sums[...], band(blocks, blocks, 0), ((1,), (0,)))
    factor = 1.0 / (window * (1.0 / (2 * RAMH * RB)) + EPS_MEAN)
    scale_blocks(raw, factor, taper, range(RAMH, blocks - RAMH + 1), normal, windowed)
    copy.wait()
    split = HOP - RAMH * RB
    rest = windowed.shape[1] - split
    ahead[...] = jnp.dot(windowed[:, split:], table[:rest, :], preferred_element_type=F32)
    behind[...] = jnp.dot(windowed[:, :split], table[HOP - split :, :], preferred_element_type=F32)


def normalize_kernel(
    slabs, raw, sums, from_even, from_odd, table, taper, ahead, behind,
    normal, to_even, to_odd, keep_right, keep_left, windowed,
):
    stations, blocks = sums.shape
    half_blocks = from_even.shape[0]
    me = lax.axis_index("tchunk")
    even = me % 2 == 0
    left = jnp.where(even, from_odd[...], from_even[...])
    right = jnp.where(even, from_even[...], from_odd[...])
    left = jnp.where(me > 0, left, 0.0)
    right = jnp.where(me < slabs - 1, right, 0.0)
    window = exact_dot(sums[...], band(blocks, blocks, 0), ((1,), (0,)))
    window += exact_dot(left, band(half_blocks, blocks, -half_blocks), ((0,), (0,)))
    window += exact_dot(right, band(half_blocks, blocks, blocks), ((0,), (0,)))
    block = lax.broadcasted_iota(jnp.int32, (stations, blocks), 1) + me * blocks
    counted = jnp.minimum(block + RAMH, slabs * blocks) - jnp.maximum(block - RAMH, 0)
    factor = 1.0 / (window / (RB * counted.astype(F32)) + EPS_MEAN)
    outer = [*range(RAMH), *range(blocks - RAMH + 1, blocks)]
    scale_blocks(raw, factor, taper, outer, normal, windowed)

    half = stations // 2
    width = NBIN // 2
    split = RAMH * RB
    rest = windowed.shape[1] - split

    sign = alternating()

    def keep(to_right, to_left):
        for n in range(table.shape[1] // width):
            here = pl.ds(n * width, width)
            right_part = jnp.dot(windowed[:, split:], table[HOP - rest :, here], preferred_element_type=F32)
            right_part += ahead[:, here]
            keep_right[:, here] = right_part[:half]
            to_right[:, here] = right_part[half:].astype(BF16)
            left_part = jnp.dot(windowed[:, :split], table[:split, here], preferred_element_type=F32)
            left_part = (left_part + behind[:, here]) * sign[:, n * width : (n + 1) * width]
            keep_left[:, here] = left_part[half:]
            to_left[:, here] = left_part[:half].astype(BF16)

    @pl.when(even)
    def _():
        keep(to_even, to_odd)

    @pl.when(jnp.logical_not(even))
    def _():
        keep(to_odd, to_even)


def whiten(spectra, nearby, scale):
    real_part = spectra[:, :NBIN]
    imag_part = spectra[:, NBIN:]
    powers = real_part * real_part + imag_part * imag_part
    high = powers.astype(BF16)
    low = (powers - high.astype(F32)).astype(BF16)
    smooth = jnp.dot(high, nearby, preferred_element_type=F32) + jnp.dot(low, nearby, preferred_element_type=F32)
    floor_level = jnp.sum(powers, axis=1, keepdims=True) * (1.0 / NBIN) + 1e-06
    inverse = lax.rsqrt(smooth * scale + LEVEL * floor_level)
    return (real_part * inverse).astype(BF16), (imag_part * inverse).astype(BF16)


def members(group, count):
    shape = (count, group.shape[1])
    return (lax.broadcasted_iota(jnp.int32, shape, 0) == group).astype(BF16)


def own_kernel(outer, middle, table, taper, group, nearby, scale, beams, windowed):
    stations = outer.shape[0]
    first = RAMH * RB
    last = first + middle.shape[1]
    parts = ((outer, 0, 0, first), (middle, 0, first, HOP), (middle, HOP - first, HOP, last), (outer, first, last, 2 * HOP))
    for source, start, low, high in parts:
        hop, inside = divmod(low, HOP)
        here = source[:, start : start + high - low].astype(F32) * taper[hop : hop + 1, inside : inside + high - low]
        windowed[hop * stations : (hop + 1) * stations, inside : inside + high - low] = here.astype(BF16)
    both = jnp.dot(windowed[...], table[...], preferred_element_type=F32)
    spectra = both[:stations] + both[stations:] * alternating()
    member = members(group[...], SUB)
    for part, white in enumerate(whiten(spectra, nearby[...], scale[...])):
        beams[part * SUB : (part + 1) * SUB, :] = jnp.dot(member, white, preferred_element_type=F32).astype(BF16)


def crossing_kernel(keep_right, keep_left, from_even, from_odd, own, group, nearby, scale, *out):
    half = keep_right.shape[0]
    held = out[-1]
    me = lax.axis_index("tchunk")
    even = me % 2 == 0
    got_even = from_even[...].astype(F32)
    got_odd = from_odd[...].astype(F32)
    ahead = keep_right[...] + jnp.where(even, got_even, got_odd)
    behind = keep_left[...] + jnp.where(even, got_odd, got_even)
    spectra = jnp.concatenate([ahead, behind], axis=0)
    station = lax.broadcasted_iota(jnp.int32, group.shape, 1)
    member = members(group[...] + jnp.where(station < half, 0, SUB), 2 * SUB)
    held[: 2 * SUB, :] = own[...]
    for part, white in enumerate(whiten(spectra, nearby[...], scale[...])):
        sums = jnp.dot(member, white, preferred_element_type=F32).astype(BF16)
        for side in range(2):
            row = (2 + 2 * side + part) * SUB
            held[row : row + SUB, :] = sums[side * SUB : (side + 1) * SUB]
    pieces = len(out) - 1
    if pieces > 1:
        width = NBIN // pieces
        for mask in range(pieces):
            start = pl.multiple_of((me ^ mask) * width, width)
            out[mask][...] = held[:, pl.ds(start, width)]
    else:
        out[0][...] = held[...]


def cross_kernel(segments, slabs, partners, *refs):
    blocks, (out, mine, others, held, done, finished) = refs[:-6], refs[-6:]
    me, home = lax.axis_index("tchunk"), lax.axis_index("stn")
    width = out.shape[1]
    rows = 6 * SUB

    def spread(target):
        for s in range(segments):
            source, after = held.at[s // 2], held.at[s // 2 + 1]
            for part in range(2):
                if s % 2 == 0:
                    target[s, part] = source[part * SUB : (part + 1) * SUB, :].astype(F32)
                else:
                    ahead = source[(2 + part) * SUB : (3 + part) * SUB, :].astype(F32)
                    behind = after[(4 + part) * SUB : (5 + part) * SUB, :].astype(F32)
                    target[s, part] = (ahead + behind).astype(BF16).astype(F32)

    for m in range(slabs):
        held[me ^ m] = blocks[0][m * rows : (m + 1) * rows, :]
    spread(mine)
    copies = []
    for slot in range(MAXP):
        partner = partners[0:1, slot : slot + 1]
        for m in range(slabs):
            chosen = jnp.zeros((rows, width), F32)
            for index in range(1, len(blocks)):
                here = blocks[index][m * rows : (m + 1) * rows, :].astype(F32)
                chosen = jnp.where(partner == home ^ index, here, chosen)
            held[me ^ m] = chosen.astype(BF16)
        spread(others)
        real, imag = [], []
        for q in range(SUB):
            real_sum = jnp.zeros((SUB, width), F32)
            imag_sum = jnp.zeros((SUB, width), F32)
            for s in range(segments):
                a, b = mine[s, 0, q : q + 1, :], mine[s, 1, q : q + 1, :]
                c, d = others[s, 0], others[s, 1]
                real_sum += a * c + b * d
                imag_sum += b * c - a * d
            real.append(real_sum * (1.0 / segments))
            imag.append(imag_sum * (1.0 / segments))
        half = SUB * SUB
        done[slot, :, :half] = jnp.transpose(jnp.concatenate(real, axis=0))
        done[slot, :, half:] = jnp.transpose(jnp.concatenate(imag, axis=0))
        copies.append(pltpu.make_async_copy(done.at[slot], out.at[slot], finished.at[slot]))
        copies[-1].start()
    for copy in copies:
        copy.wait()


def body(raw_data, station_group, partner_blocks):
    stations, samples = raw_data.shape
    slabs = lax.axis_size("tchunk")
    count_blocks = lax.axis_size("stn")
    me, home = lax.axis_index("tchunk"), lax.axis_index("stn")
    blocks = samples // RB
    half = stations // 2
    table, taper = (jnp.asarray(t) for t in dft_tables())
    nearby, scale = (jnp.asarray(t) for t in smooth_tables())
    group = station_group[None, :]
    shape = jax.ShapeDtypeStruct

    halo = shape((blocks // 2, stations), F32)
    in_hbm = [pltpu.with_memory_space_constraint(a, pltpu.HBM) for a in (raw_data, taper, table)]
    raw, sums, even, odd, taper = call(
        sums_kernel,
        (shape(raw_data.shape, F32), shape((stations, blocks), F32), halo, halo, shape(taper.shape, F32)),
        in_hbm[:2],
        specs=[HBM, HBM],
        scratch_shapes=[pltpu.VMEM((stations, RB), F32), pltpu.SemaphoreType.DMA((4,))],
        flops=2 * stations * samples,
    )
    even, odd = neighbour_swap(even, odd)
    sent = shape((half, 2 * NBIN), BF16)
    kept = shape((half, 2 * NBIN), F32)
    inner = (blocks - 2 * RAMH + 1) * RB
    partial = shape((stations, 2 * NBIN), F32)
    table, middle, ahead, behind = call(
        middle_kernel,
        (shape(table.shape, BF16), shape((stations, inner), BF16), partial, partial),
        (raw, sums, in_hbm[2], taper),
        specs=[VMEM, VMEM, HBM, VMEM],
        scratch_shapes=[pltpu.VMEM((stations, inner), BF16), pltpu.SemaphoreType.DMA],
        flops=4 * stations * inner * NBIN,
    )
    edge = shape((stations, samples - inner), BF16)
    outer, even, odd, keep_right, keep_left = call(
        functools.partial(normalize_kernel, slabs),
        (edge, sent, sent, kept, kept),
        (raw, sums, even, odd, table, taper, ahead, behind),
        scratch_shapes=[pltpu.VMEM(edge.shape, BF16)],
        flops=4 * stations * samples * NBIN,
        limit=16,
    )
    even, odd = neighbour_swap(even, odd)
    own = call(
        own_kernel,
        shape((2 * SUB, NBIN), BF16),
        (outer, middle, table, taper, group, nearby, scale),
        scratch_shapes=[pltpu.VMEM((2 * stations, HOP), BF16)],
        flops=4 * stations * samples * NBIN,
        limit=32,
    )
    direct = slabs <= 8 and slabs & (slabs - 1) == 0 and NBIN // slabs % 128 == 0
    width = NBIN // slabs
    rows = 6 * SUB
    pieces = call(
        crossing_kernel,
        tuple([shape((rows, width), BF16)] * slabs) if direct else (shape((rows, NBIN), BF16),),
        (keep_right, keep_left, even, odd, own, group, nearby, scale),
        scratch_shapes=[pltpu.VMEM((rows, NBIN), BF16)],
        flops=8 * stations * NBIN * NBIN,
        limit=32,
    )
    if direct:
        order = sorted(range(1, slabs), key=lambda m: (m % 2 == 0, m))
        received = {m: swapped(pieces[m], "tchunk", m) for m in order}
        mine = jnp.concatenate([pieces[0]] + [received[m] for m in range(1, slabs)], axis=0)
    else:
        mine = pieces[0].reshape(rows, slabs, width).swapaxes(0, 1)
        mine = lax.all_to_all(mine, "tchunk", split_axis=0, concat_axis=0, tiled=True)
        mine = mine[jnp.arange(slabs) ^ me].reshape(slabs * rows, width)
    segments = SEG_DEV * slabs - 1
    if count_blocks == 4:
        across = swapped(mine, "stn", 2)
        others = [mine, swapped(mine, "stn", 1), across, swapped(across, "stn", 1)]
    else:
        gathered = lax.all_gather(mine, "stn", axis=0)
        others = [lax.dynamic_index_in_dim(gathered, home ^ m, 0, keepdims=False) for m in range(count_blocks)]
    result = (MAXP, width, 2 * SUB * SUB)
    out = call(
        functools.partial(cross_kernel, segments, slabs),
        shape(result, F32),
        (partner_blocks, *others),
        out_specs=HBM,
        scratch_shapes=[pltpu.VMEM((segments, 2, SUB, width), F32)] * 2
        + [pltpu.VMEM((slabs, rows, width), BF16), pltpu.VMEM(result, F32), pltpu.SemaphoreType.DMA((MAXP,))],
        flops=MAXP * segments * width * SUB * SUB * 8,
        limit=32,
    )
    return out[None]


def solution(mesh):
    placed = (P("stn", ("hour", "tchunk")), P("stn"), P("stn", None))
    return jax.shard_map(
        body,
        mesh=mesh,
        in_specs=placed,
        out_specs=P(("hour", "stn"), None, "tchunk", None),
        check_vma=False,
    )
```

```python
import functools
import math

import jax
import jax.numpy as jnp
import ml_dtypes
import numpy as np
from jax import lax
from jax.experimental import pallas as pl
from jax.experimental.pallas import tpu as pltpu
from jax.sharding import PartitionSpec as P

SEG_DEV = 2
SEGLEN = 4096
HOP = 2048
NBIN = 512
RB = 128
RAMH = 10
SMOOTH = 8
SUB = 16
MAXP = 3

EPS_MEAN = 1e-06
LEVEL = 0.05

BF16 = jnp.bfloat16
F32 = jnp.float32
VMEM = pl.BlockSpec(memory_space=pltpu.VMEM)
HBM = pl.BlockSpec(memory_space=pltpu.HBM)
MIB = 1 << 20


def dft_tables():
    sample = np.arange(HOP, dtype=np.int32)
    frequency = np.arange(1, NBIN + 1, dtype=np.int32)
    turn = np.arange(SEGLEN, dtype=np.float64) * (2.0 * math.pi / SEGLEN)
    phases = sample[:, None] * frequency[None, :] % SEGLEN
    matrix = np.concatenate([np.cos(turn)[phases], -np.sin(turn)[phases]], axis=1)
    taper = (0.5 - 0.5 * np.cos(turn)).reshape(2, HOP)
    matrix = matrix.astype(np.float32).astype(ml_dtypes.bfloat16)
    return matrix, taper.astype(np.float32)


def smooth_tables():
    bin_index = np.arange(NBIN)
    nearby = np.abs(bin_index[:, None] - bin_index[None, :]) <= SMOOTH
    scale = 1.0 / np.sum(nearby, axis=0, keepdims=True)
    return nearby.astype(ml_dtypes.bfloat16), scale.astype(np.float32)


def neighbour_swap(first, second, outer_first):
    blocks, slabs = lax.axis_size("stn"), lax.axis_size("tchunk")
    inner = [(i, i ^ 1) for i in range(slabs - slabs % 2)]
    outer = [(i, i + 1) for i in range(1, slabs - 1, 2)]
    outer += [(j, i) for i, j in outer]
    pairs = [[(b * slabs + i, b * slabs + j) for b in range(blocks) for i, j in part] for part in (inner, outer)]
    if blocks % 2 == 0 and slabs % 2 == 0:
        pairs[1] += [(b * slabs + i, (b ^ 1) * slabs + i) for b in range(blocks) for i in (0, slabs - 1)]
    sent = {}
    for i in (1, 0) if outer_first else (0, 1):
        sent[i] = lax.ppermute((first, second)[i], ("stn", "tchunk"), pairs[i])
    return sent[0], sent[1]


def swapped(block, axis, mask):
    return lax.ppermute(block, axis, [(i, i ^ mask) for i in range(lax.axis_size(axis))])


def call(kernel, out_shape, operands, specs=None, flops=0, limit=16, **more):
    moved = sum(math.prod(a.shape) * a.dtype.itemsize for a in list(operands) + jax.tree.leaves(out_shape))
    more.setdefault("out_specs", jax.tree.map(lambda _: VMEM, out_shape))
    return pl.pallas_call(
        kernel,
        out_shape=out_shape,
        in_specs=specs or [VMEM] * len(operands),
        compiler_params=pltpu.CompilerParams(vmem_limit_bytes=limit * MIB),
        cost_estimate=pl.CostEstimate(flops=flops, bytes_accessed=moved, transcendentals=0),
        **more,
    )(*operands)


def sums_kernel(source, taper_source, raw, sums, to_even, to_odd, taper, held, arrived):
    chunks = arrived.shape[0] - 1
    stations, samples = raw.shape
    blocks = samples // RB
    ends = [stations * n // 9 // 8 * 8 for n in (0, 3, 6, 9)]
    copies = []
    for step in range(chunks):
        rows = ends[step + 1] - ends[step]
        here = pl.ds(ends[step], rows)
        copies.append(pltpu.make_async_copy(source.at[here], raw.at[here], arrived.at[step]))
        copies[-1].start()
    copies.append(pltpu.make_async_copy(taper_source, taper, arrived.at[chunks]))
    copies[-1].start()
    for step in range(chunks):
        copies[step].wait()
        rows = ends[step + 1] - ends[step]
        here = pl.ds(ends[step], rows)
        lane = lax.broadcasted_iota(jnp.int32, (rows, RB), 1)
        total = jnp.zeros((rows, RB), F32)
        for b in range(blocks):
            amount = jnp.sum(jnp.abs(raw[here, b * RB : (b + 1) * RB]), axis=1, keepdims=True)
            total = jnp.where(lane == b, amount, total)
        held[here, :] = total
    whole = held[...]
    sums[...] = whole[:, :blocks]
    flipped = jnp.transpose(whole)
    head = flipped[: blocks // 2]
    tail = flipped[blocks // 2 : blocks]
    even = lax.axis_index("tchunk") % 2 == 0
    to_even[...] = jnp.where(even, tail, head)
    to_odd[...] = jnp.where(even, head, tail)
    copies[-1].wait()


def split_dot(left, right, axis):
    high = left.astype(BF16)
    rest = left - high.astype(F32)
    middle = rest.astype(BF16)
    low = (rest - middle.astype(F32)).astype(BF16)
    parts = jnp.concatenate([high, middle, low], axis=axis)
    return lax.dot_general(
        parts, jnp.concatenate([right] * 3, axis=0), (((axis,), (0,)), ((), ())), preferred_element_type=F32
    )


def band(rows, blocks, first):
    source = lax.broadcasted_iota(jnp.int32, (rows, blocks), 0) + first
    target = lax.broadcasted_iota(jnp.int32, (rows, blocks), 1)
    return ((source >= target - RAMH) & (source < target + RAMH)).astype(BF16)


def alternating():
    column = lax.broadcasted_iota(jnp.int32, (1, 2 * NBIN), 1)
    return jnp.where(column % 2 == 0, -1.0, 1.0)


def windowed_blocks(raw, factor, taper, rows, some, normal, windowed):
    for place, b in enumerate(some):
        here = pl.ds(place * RB, RB)
        scaled = (raw[rows, b * RB : (b + 1) * RB] * factor[rows, b : b + 1]).astype(BF16)
        if normal is not None:
            normal[:, here] = scaled
        hop, inside = divmod(b * RB, HOP)
        weight = taper[1 - hop : 2 - hop, inside : inside + RB]
        windowed[:, here] = (scaled.astype(F32) * weight).astype(BF16)


def middle_kernel(raw, sums, table, taper, normal, ahead, behind, window, windowed):
    blocks = sums.shape[1]
    window[...] = split_dot(sums[...], band(blocks, blocks, 0), 1)
    factor = 1.0 / (window[...] * (1.0 / (2 * RAMH * RB)) + EPS_MEAN)
    windowed_blocks(raw, factor, taper, slice(None), range(RAMH, blocks - RAMH + 1), normal, windowed)
    split = HOP - RAMH * RB
    rest = windowed.shape[1] - split
    ahead[...] = jnp.dot(windowed[:, split:], table[:rest, :], preferred_element_type=F32)
    behind[...] = jnp.dot(windowed[:, :split], table[HOP - split :, :], preferred_element_type=F32)


def send_kernel(
    slabs, raw, window, from_odd, from_even, table, taper, ahead, behind,
    to_even, to_odd, factor, first, last,
):
    stations, blocks = window.shape
    half_blocks = from_even.shape[0]
    half = stations // 2
    me = lax.axis_index("tchunk")
    even = me % 2 == 0
    left = jnp.where(even, from_odd[...], from_even[...])
    right = jnp.where(even, from_even[...], from_odd[...])
    left = jnp.where(me > 0, left, 0.0)
    right = jnp.where(me < slabs - 1, right, 0.0)
    near = jnp.concatenate([left, right], axis=0)
    bands = jnp.concatenate([band(half_blocks, blocks, -half_blocks), band(half_blocks, blocks, blocks)], axis=0)
    total = window[...] + split_dot(near, bands, 0)
    block = lax.broadcasted_iota(jnp.int32, (stations, blocks), 1) + me * blocks
    counted = jnp.minimum(block + RAMH, slabs * blocks) - jnp.maximum(block - RAMH, 0)
    factor[...] = 1.0 / (total / (RB * counted.astype(F32)) + EPS_MEAN)
    windowed_blocks(raw, factor, taper, slice(half, stations), range(blocks - RAMH + 1, blocks), None, last)
    windowed_blocks(raw, factor, taper, slice(0, half), range(RAMH), None, first)
    sign = alternating()
    width = NBIN // 2

    def fill(to_right, to_left):
        for n in range(table.shape[1] // width):
            here = slice(n * width, (n + 1) * width)
            part = jnp.dot(last[...], table[HOP - last.shape[1] :, here], preferred_element_type=F32)
            to_right[:, here] = (part + ahead[half:, here]).astype(BF16)
            part = jnp.dot(first[...], table[: first.shape[1], here], preferred_element_type=F32)
            to_left[:, here] = ((part + behind[:half, here]) * sign[:, here]).astype(BF16)

    @pl.when(even)
    def _():
        fill(to_even, to_odd)

    @pl.when(jnp.logical_not(even))
    def _():
        fill(to_odd, to_even)


def whiten(spectra, nearby, scale):
    real_part = spectra[:, :NBIN]
    imag_part = spectra[:, NBIN:]
    powers = real_part * real_part + imag_part * imag_part
    high = powers.astype(BF16)
    low = (powers - high.astype(F32)).astype(BF16)
    smooth = jnp.dot(high, nearby, preferred_element_type=F32) + jnp.dot(low, nearby, preferred_element_type=F32)
    floor_level = jnp.sum(powers, axis=1, keepdims=True) * (1.0 / NBIN) + 1e-06
    inverse = lax.rsqrt(smooth * scale + LEVEL * floor_level)
    return (real_part * inverse).astype(BF16), (imag_part * inverse).astype(BF16)


def members(group, count):
    shape = (count, group.shape[1])
    return (lax.broadcasted_iota(jnp.int32, shape, 0) == group).astype(BF16)


def own_kernel(
    raw, factor, middle, table, taper, ahead, behind, group, nearby, scale,
    beams, keep_right, keep_left, windowed, first, last,
):
    stations, blocks = factor.shape
    half = stations // 2
    windowed_blocks(raw, factor, taper, slice(0, half), range(blocks - RAMH + 1, blocks), None, last)
    windowed_blocks(raw, factor, taper, slice(half, stations), range(RAMH), None, first)
    part = jnp.dot(last[...], table[HOP - last.shape[1] :, :], preferred_element_type=F32)
    keep_right[...] = part + ahead[:half]
    part = jnp.dot(first[...], table[: first.shape[1], :], preferred_element_type=F32)
    keep_left[...] = (part + behind[half:]) * alternating()

    for b in range(blocks):
        hop, inside = divmod(b * RB, HOP)
        if RAMH <= b <= blocks - RAMH:
            scaled = middle[:, (b - RAMH) * RB : (b - RAMH + 1) * RB]
        else:
            scaled = (raw[:, b * RB : (b + 1) * RB] * factor[:, b : b + 1]).astype(BF16)
        weight = taper[hop : hop + 1, inside : inside + RB]
        rows = slice(hop * stations, (hop + 1) * stations)
        windowed[rows, inside : inside + RB] = (scaled.astype(F32) * weight).astype(BF16)
    both = jnp.dot(windowed[...], table[...], preferred_element_type=F32)
    spectra = both[:stations] + both[stations:] * alternating()
    member = members(group[...], SUB)
    for part, white in enumerate(whiten(spectra, nearby[...], scale[...])):
        beams[part * SUB : (part + 1) * SUB, :] = jnp.dot(member, white, preferred_element_type=F32).astype(BF16)


def crossing_kernel(keep_right, keep_left, from_even, from_odd, own, group, nearby, scale, *out):
    half = keep_right.shape[0]
    held = out[-1]
    me = lax.axis_index("tchunk")
    even = me % 2 == 0
    got_even = from_even[...].astype(F32)
    got_odd = from_odd[...].astype(F32)
    ahead = keep_right[...] + jnp.where(even, got_even, got_odd)
    behind = keep_left[...] + jnp.where(even, got_odd, got_even)
    spectra = jnp.concatenate([ahead, behind], axis=0)
    station = lax.broadcasted_iota(jnp.int32, group.shape, 1)
    member = members(group[...] + jnp.where(station < half, 0, SUB), 2 * SUB)
    held[: 2 * SUB, :] = own[...]
    for part, white in enumerate(whiten(spectra, nearby[...], scale[...])):
        sums = jnp.dot(member, white, preferred_element_type=F32).astype(BF16)
        for side in range(2):
            row = (2 + 2 * side + part) * SUB
            held[row : row + SUB, :] = sums[side * SUB : (side + 1) * SUB]
    pieces = len(out) - 1
    if pieces > 1:
        width = NBIN // pieces
        for mask in range(pieces):
            start = pl.multiple_of((me ^ mask) * width, width)
            out[mask][...] = held[:, pl.ds(start, width)]
    else:
        out[0][...] = held[...]


def far_first(slabs):
    return [0, *range(slabs - 1, 0, -1)]


def combine_kernel(segments, slabs, *refs):
    pieces, (out, held) = refs[:-2], refs[-2:]
    me = lax.axis_index("tchunk")
    side = 2 * SUB
    order = far_first(slabs)
    for m in range(slabs):
        if len(pieces) == slabs:
            held[me ^ order[m]] = pieces[m][...].astype(F32)
        else:
            held[m] = pieces[0][m].astype(F32)
    for s in range(segments):
        here = held[s // 2, :side, :]
        if s % 2 == 1:
            here = held[s // 2, side : 2 * side, :] + held[s // 2 + 1, 2 * side :, :]
        out[s * side : (s + 1) * side, :] = here.astype(BF16)


def cross_terms(segments, mine, others, out):
    side = 2 * SUB
    real, imag = [], []
    for q in range(SUB):
        real_sum = jnp.zeros((SUB, mine.shape[1]), F32)
        imag_sum = jnp.zeros((SUB, mine.shape[1]), F32)
        for s in range(segments):
            first = s * side
            a, b = mine[first + q : first + q + 1, :], mine[first + SUB + q : first + SUB + q + 1, :]
            c, d = others[first : first + SUB, :], others[first + SUB : first + side, :]
            real_sum += a * c + b * d
            imag_sum += b * c - a * d
        real.append(real_sum * (1.0 / segments))
        imag.append(imag_sum * (1.0 / segments))
    half = SUB * SUB
    out[:, :half] = jnp.transpose(jnp.concatenate(real, axis=0))
    out[:, half:] = jnp.transpose(jnp.concatenate(imag, axis=0))


def near_kernel(segments, own, *refs):
    blocks, (products, mine, others) = refs[:-3], refs[-3:]
    mine[...] = own[...].astype(F32)
    products[0] = jnp.zeros(products.shape[1:], F32)
    for index, block in enumerate(blocks):
        others[...] = block[...].astype(F32)
        cross_terms(segments, mine, others, products.at[index + 1])


def last_kernel(segments, partners, own, block, products, out, mine, others, last, finished):
    home = lax.axis_index("stn")
    count = products.shape[0]
    which = []
    for slot in range(MAXP):
        partner = jnp.max(partners[0:1, slot : slot + 1])
        which.append(jnp.where(partner < 0, 0, partner ^ home))

    def copy(slot, source):
        return pltpu.make_async_copy(source, out.at[slot], finished.at[slot])

    for slot in range(MAXP):
        @pl.when(which[slot] < count)
        def _(slot=slot):
            copy(slot, products.at[jnp.minimum(which[slot], count - 1)]).start()

    mine[...] = own[...].astype(F32)
    others[...] = block[...].astype(F32)
    cross_terms(segments, mine, others, last)
    for slot in range(MAXP):
        @pl.when(which[slot] >= count)
        def _(slot=slot):
            copy(slot, last).start()

    for slot in range(MAXP):
        copy(slot, last).wait()


def cross_kernel(segments, partners, *refs):
    blocks, (out, mine, others, done, finished) = refs[:-5], refs[-5:]
    home = lax.axis_index("stn")
    mine[...] = blocks[0][...].astype(F32)
    copies = []
    for slot in range(MAXP):
        partner = partners[0:1, slot : slot + 1]
        chosen = jnp.zeros(mine.shape, F32)
        for index in range(1, len(blocks)):
            chosen = jnp.where(partner == home ^ index, blocks[index][...].astype(F32), chosen)
        others[...] = chosen
        cross_terms(segments, mine, others, done.at[slot])
        copies.append(pltpu.make_async_copy(done.at[slot], out.at[slot], finished.at[slot]))
        copies[-1].start()
    for copy in copies:
        copy.wait()


def body(raw_data, station_group, partner_blocks):
    stations, samples = raw_data.shape
    slabs = lax.axis_size("tchunk")
    count_blocks = lax.axis_size("stn")
    me, home = lax.axis_index("tchunk"), lax.axis_index("stn")
    blocks = samples // RB
    half = stations // 2
    table, taper = (jnp.asarray(t) for t in dft_tables())
    nearby, scale = (jnp.asarray(t) for t in smooth_tables())
    group = station_group[None, :]
    shape = jax.ShapeDtypeStruct

    halo = shape((blocks // 2, stations), F32)
    in_hbm = [pltpu.with_memory_space_constraint(a, pltpu.HBM) for a in (raw_data, taper, table)]
    raw, sums, even, odd, taper = call(
        sums_kernel,
        (shape(raw_data.shape, F32), shape((stations, blocks), F32), halo, halo, shape(taper.shape, F32)),
        in_hbm[:2],
        specs=[HBM, HBM],
        scratch_shapes=[pltpu.VMEM((stations, RB), F32), pltpu.SemaphoreType.DMA((4,))],
        flops=10**10,
    )
    even, odd = neighbour_swap(even, odd, True)
    sent = shape((half, 2 * NBIN), BF16)
    kept = shape((half, 2 * NBIN), F32)
    inner = (blocks - 2 * RAMH + 1) * RB
    partial = shape((stations, 2 * NBIN), F32)
    middle, ahead, behind, window = call(
        middle_kernel,
        (shape((stations, inner), BF16), partial, partial, shape((stations, blocks), F32)),
        (raw, sums, table, taper),
        scratch_shapes=[pltpu.VMEM((stations, inner), BF16)],
        flops=4 * stations * inner * NBIN,
    )
    edges = [pltpu.VMEM((half, RAMH * RB), BF16), pltpu.VMEM((half, (RAMH - 1) * RB), BF16)]
    even, odd, factor = call(
        functools.partial(send_kernel, slabs),
        (sent, sent, shape((stations, blocks), F32)),
        (raw, window, odd, even, table, taper, ahead, behind),
        scratch_shapes=edges,
        flops=2 * stations * samples * NBIN,
    )
    even, odd = neighbour_swap(even, odd, False)
    own, keep_right, keep_left = call(
        own_kernel,
        (shape((2 * SUB, NBIN), BF16), kept, kept),
        (raw, factor, middle, table, taper, ahead, behind, group, nearby, scale),
        scratch_shapes=[pltpu.VMEM((2 * stations, HOP), BF16), *edges],
        flops=6 * stations * samples * NBIN,
    )
    direct = slabs <= 8 and slabs & (slabs - 1) == 0 and NBIN // slabs % 128 == 0
    width = NBIN // slabs
    rows = 6 * SUB
    pieces = call(
        crossing_kernel,
        tuple([shape((rows, width), BF16)] * slabs) if direct else (shape((rows, NBIN), BF16),),
        (keep_right, keep_left, even, odd, own, group, nearby, scale),
        scratch_shapes=[pltpu.VMEM((rows, NBIN), BF16)],
        flops=8 * stations * NBIN * NBIN,
        limit=32,
    )
    if direct:
        order = far_first(slabs)[1:]
        received = {m: swapped(pieces[m], "tchunk", m) for m in order}
        received = [pieces[0]] + [received[m] for m in far_first(slabs)[1:]]
    else:
        received = pieces[0].reshape(rows, slabs, width).swapaxes(0, 1)
        received = [lax.all_to_all(received, "tchunk", split_axis=0, concat_axis=0, tiled=True)]
    segments = SEG_DEV * slabs - 1
    mine = call(
        functools.partial(combine_kernel, segments, slabs),
        shape((segments * 2 * SUB, width), BF16),
        received,
        scratch_shapes=[pltpu.VMEM((slabs, rows, width), F32)],
    )
    result = (MAXP, width, 2 * SUB * SUB)
    floats = [pltpu.VMEM(mine.shape, F32)] * 2
    flops = segments * width * SUB * SUB * 8
    if count_blocks == 4:
        across = swapped(mine, "stn", 2)
        beside = swapped(mine, "stn", 1)
        last = swapped(across, "stn", 1)
        products = call(
            functools.partial(near_kernel, segments),
            shape(result, F32),
            (mine, beside, across),
            scratch_shapes=floats,
            flops=2 * flops,
        )
        out = call(
            functools.partial(last_kernel, segments),
            shape(result, F32),
            (partner_blocks, mine, last, products),
            out_specs=HBM,
            scratch_shapes=floats + [pltpu.VMEM(result[1:], F32), pltpu.SemaphoreType.DMA((MAXP,))],
            flops=flops,
        )
    else:
        gathered = lax.all_gather(mine, "stn", axis=0)
        others = [lax.dynamic_index_in_dim(gathered, home ^ m, 0, keepdims=False) for m in range(count_blocks)]
        out = call(
            functools.partial(cross_kernel, segments),
            shape(result, F32),
            (partner_blocks, *others),
            out_specs=HBM,
            scratch_shapes=floats + [pltpu.VMEM(result, F32), pltpu.SemaphoreType.DMA((MAXP,))],
            flops=MAXP * flops,
            limit=32,
        )
    return out[None]


def solution(mesh):
    placed = (P("stn", ("hour", "tchunk")), P("stn"), P("stn", None))
    return jax.shard_map(
        body,
        mesh=mesh,
        in_specs=placed,
        out_specs=P(("hour", "stn"), None, "tchunk", None),
        check_vma=False,
    )
```

```python
import functools
import math

import jax
import jax.numpy as jnp
import ml_dtypes
import numpy as np
from jax import lax
from jax.experimental import pallas as pl
from jax.experimental.pallas import tpu as pltpu
from jax.sharding import PartitionSpec as P

SEG_DEV = 2
SEGLEN = 4096
HOP = 2048
NBIN = 512
RB = 128
RAMH = 10
SMOOTH = 8
SUB = 16
MAXP = 3

EPS_MEAN = 1e-06
LEVEL = 0.05

BF16 = jnp.bfloat16
F32 = jnp.float32
VMEM = pl.BlockSpec(memory_space=pltpu.VMEM)
HBM = pl.BlockSpec(memory_space=pltpu.HBM)
MIB = 1 << 20


def dft_tables():
    sample = np.arange(HOP, dtype=np.int32)
    frequency = np.arange(1, NBIN + 1, dtype=np.int32)
    turn = np.arange(SEGLEN, dtype=np.float64) * (2.0 * math.pi / SEGLEN)
    phases = sample[:, None] * frequency[None, :] % SEGLEN
    matrix = np.concatenate([np.cos(turn)[phases], -np.sin(turn)[phases]], axis=1)
    taper = (0.5 - 0.5 * np.cos(turn)).reshape(2, HOP)
    repeated = np.concatenate([matrix, matrix * np.concatenate([(-1.0) ** frequency] * 2)], axis=0)
    tapered = (taper.reshape(-1, 1) * repeated).astype(np.float32).astype(ml_dtypes.bfloat16)
    matrix = matrix.astype(np.float32).astype(ml_dtypes.bfloat16)
    return tapered, matrix, taper.astype(np.float32)


def smooth_tables():
    bin_index = np.arange(NBIN)
    nearby = np.abs(bin_index[:, None] - bin_index[None, :]) <= SMOOTH
    scale = 1.0 / np.sum(nearby, axis=0, keepdims=True)
    return nearby.astype(ml_dtypes.bfloat16), scale.astype(np.float32)


def neighbour_swap(first, second, outer_first):
    blocks, slabs = lax.axis_size("stn"), lax.axis_size("tchunk")
    inner = [(i, i ^ 1) for i in range(slabs - slabs % 2)]
    outer = [(i, i + 1) for i in range(1, slabs - 1, 2)]
    outer += [(j, i) for i, j in outer]
    pairs = [[(b * slabs + i, b * slabs + j) for b in range(blocks) for i, j in part] for part in (inner, outer)]
    if blocks % 2 == 0 and slabs % 2 == 0:
        pairs[1] += [(b * slabs + i, (b ^ 1) * slabs + i) for b in range(blocks) for i in (0, slabs - 1)]
    sent = {}
    for i in (1, 0) if outer_first else (0, 1):
        sent[i] = lax.ppermute((first, second)[i], ("stn", "tchunk"), pairs[i])
    return sent[0], sent[1]


def swapped(block, axis, mask):
    return lax.ppermute(block, axis, [(i, i ^ mask) for i in range(lax.axis_size(axis))])


def call(kernel, out_shape, operands, specs=None, flops=0, limit=16, **more):
    moved = sum(math.prod(a.shape) * a.dtype.itemsize for a in list(operands) + jax.tree.leaves(out_shape))
    more.setdefault("out_specs", jax.tree.map(lambda _: VMEM, out_shape))
    return pl.pallas_call(
        kernel,
        out_shape=out_shape,
        in_specs=specs or [VMEM] * len(operands),
        compiler_params=pltpu.CompilerParams(vmem_limit_bytes=limit * MIB),
        cost_estimate=pl.CostEstimate(flops=flops, bytes_accessed=moved, transcendentals=0),
        **more,
    )(*operands)


def sums_kernel(source, taper_source, raw, sums, to_even, to_odd, taper, held, arrived):
    chunks = arrived.shape[0] - 1
    stations, samples = raw.shape
    blocks = samples // RB
    ends = [stations * n // 9 // 8 * 8 for n in (0, 3, 6, 9)]
    copies = []
    for step in range(chunks):
        rows = ends[step + 1] - ends[step]
        here = pl.ds(ends[step], rows)
        copies.append(pltpu.make_async_copy(source.at[here], raw.at[here], arrived.at[step]))
        copies[-1].start()
    copies.append(pltpu.make_async_copy(taper_source, taper, arrived.at[chunks]))
    copies[-1].start()
    for step in range(chunks):
        copies[step].wait()
        rows = ends[step + 1] - ends[step]
        here = pl.ds(ends[step], rows)
        lane = lax.broadcasted_iota(jnp.int32, (rows, RB), 1)
        total = jnp.zeros((rows, RB), F32)
        for b in range(blocks):
            amount = jnp.sum(jnp.abs(raw[here, b * RB : (b + 1) * RB]), axis=1, keepdims=True)
            total = jnp.where(lane == b, amount, total)
        held[here, :] = total
    whole = held[...]
    sums[...] = whole[:, :blocks]
    flipped = jnp.transpose(whole)
    head = flipped[: blocks // 2]
    tail = flipped[blocks // 2 : blocks]
    even = lax.axis_index("tchunk") % 2 == 0
    to_even[...] = jnp.where(even, tail, head)
    to_odd[...] = jnp.where(even, head, tail)
    copies[-1].wait()


def split_dot(left, right, axis):
    high = left.astype(BF16)
    rest = left - high.astype(F32)
    middle = rest.astype(BF16)
    low = (rest - middle.astype(F32)).astype(BF16)
    parts = jnp.concatenate([high, middle, low], axis=axis)
    return lax.dot_general(
        parts, jnp.concatenate([right] * 3, axis=0), (((axis,), (0,)), ((), ())), preferred_element_type=F32
    )


def band(rows, blocks, first):
    source = lax.broadcasted_iota(jnp.int32, (rows, blocks), 0) + first
    target = lax.broadcasted_iota(jnp.int32, (rows, blocks), 1)
    return ((source >= target - RAMH) & (source < target + RAMH)).astype(BF16)


def alternating():
    column = lax.broadcasted_iota(jnp.int32, (1, 2 * NBIN), 1)
    return jnp.where(column % 2 == 0, -1.0, 1.0)


def windowed_blocks(raw, factor, taper, rows, some, normal, windowed):
    for place, b in enumerate(some):
        here = pl.ds(place * RB, RB)
        scaled = (raw[rows, b * RB : (b + 1) * RB] * factor[rows, b : b + 1]).astype(BF16)
        if normal is not None:
            normal[:, here] = scaled
        hop, inside = divmod(b * RB, HOP)
        weight = taper[1 - hop : 2 - hop, inside : inside + RB]
        windowed[:, here] = (scaled.astype(F32) * weight).astype(BF16)


def middle_kernel(raw, sums, table, taper, normal, ahead, behind, window, last, first, windowed, bare):
    blocks = sums.shape[1]
    half = raw.shape[0] // 2
    for source, rows, some, out in (
        (raw, slice(half, None), range(blocks - RAMH + 1, blocks), last),
        (raw, slice(0, half), range(RAMH), first),
    ):
        for place, b in enumerate(some):
            hop, inside = divmod(b * RB, HOP)
            weight = taper[1 - hop : 2 - hop, inside : inside + RB]
            bare[place] = (source[rows, b * RB : (b + 1) * RB] * weight).astype(BF16)
            out[place] = jnp.dot(bare[place], table[inside : inside + RB, :], preferred_element_type=F32)

    window[...] = split_dot(sums[...], band(blocks, blocks, 0), 1)
    factor = 1.0 / (window[...] * (1.0 / (2 * RAMH * RB)) + EPS_MEAN)
    windowed_blocks(raw, factor, taper, slice(None), range(RAMH, blocks - RAMH + 1), normal, windowed)
    split = HOP - RAMH * RB
    rest = windowed.shape[1] - split
    ahead[...] = jnp.dot(windowed[:, split:], table[:rest, :], preferred_element_type=F32)
    behind[...] = jnp.dot(windowed[:, :split], table[HOP - split :, :], preferred_element_type=F32)


def send_kernel(slabs, window, from_odd, from_even, ahead, behind, last, first, to_even, to_odd, factor):
    stations, blocks = window.shape
    half_blocks = from_even.shape[0]
    half = stations // 2
    me = lax.axis_index("tchunk")
    even = me % 2 == 0
    left = jnp.where(even, from_odd[...], from_even[...])
    right = jnp.where(even, from_even[...], from_odd[...])
    left = jnp.where(me > 0, left, 0.0)
    right = jnp.where(me < slabs - 1, right, 0.0)
    near = jnp.concatenate([left, right], axis=0)
    bands = jnp.concatenate([band(half_blocks, blocks, -half_blocks), band(half_blocks, blocks, blocks)], axis=0)
    total = window[...] + split_dot(near, bands, 0)
    block = lax.broadcasted_iota(jnp.int32, (stations, blocks), 1) + me * blocks
    counted = jnp.minimum(block + RAMH, slabs * blocks) - jnp.maximum(block - RAMH, 0)
    factor[...] = 1.0 / (total / (RB * counted.astype(F32)) + EPS_MEAN)
    sign = alternating()
    width = NBIN

    def fill(to_right, to_left):
        for n in range(ahead.shape[1] // width):
            here = slice(n * width, (n + 1) * width)
            part = ahead[half:, here]
            for place in range(RAMH - 1):
                b = blocks - RAMH + 1 + place
                part += factor[half:, b : b + 1] * last[place, :, here]
            to_right[:, here] = part.astype(BF16)
            part = behind[:half, here]
            for b in range(RAMH):
                part += factor[:half, b : b + 1] * first[b, :, here]
            to_left[:, here] = (part * sign[:, here]).astype(BF16)

    @pl.when(even)
    def _():
        fill(to_even, to_odd)

    @pl.when(jnp.logical_not(even))
    def _():
        fill(to_odd, to_even)


def whiten(spectra, nearby, scale):
    real_part = spectra[:, :NBIN]
    imag_part = spectra[:, NBIN:]
    powers = real_part * real_part + imag_part * imag_part
    high = powers.astype(BF16)
    low = (powers - high.astype(F32)).astype(BF16)
    smooth = jnp.dot(high, nearby, preferred_element_type=F32) + jnp.dot(low, nearby, preferred_element_type=F32)
    floor_level = jnp.sum(powers, axis=1, keepdims=True) * (1.0 / NBIN) + 1e-06
    inverse = lax.rsqrt(smooth * scale + LEVEL * floor_level)
    return (real_part * inverse).astype(BF16), (imag_part * inverse).astype(BF16)


def members(group, count):
    shape = (count, group.shape[1])
    return (lax.broadcasted_iota(jnp.int32, shape, 0) == group).astype(BF16)


def own_kernel(
    raw, factor, middle, table, tapered, taper, ahead, behind, group, nearby, scale,
    beams, keep_right, keep_left, normal, first, last,
):
    stations, blocks = factor.shape
    half = stations // 2
    windowed_blocks(raw, factor, taper, slice(0, half), range(blocks - RAMH + 1, blocks), None, last)
    windowed_blocks(raw, factor, taper, slice(half, stations), range(RAMH), None, first)
    part = jnp.dot(last[...], table[HOP - last.shape[1] :, :], preferred_element_type=F32)
    keep_right[...] = part + ahead[:half]
    part = jnp.dot(first[...], table[: first.shape[1], :], preferred_element_type=F32)
    keep_left[...] = (part + behind[half:]) * alternating()

    for b in [*range(RAMH), *range(blocks - RAMH + 1, blocks)]:
        here = pl.ds(b * RB, RB)
        normal[:, here] = (raw[:, here] * factor[:, b : b + 1]).astype(BF16)
    normal[:, RAMH * RB : RAMH * RB + middle.shape[1]] = middle[...]
    spectra = jnp.dot(normal[...], tapered[...], preferred_element_type=F32)
    member = members(group[...], SUB)
    for part, white in enumerate(whiten(spectra, nearby[...], scale[...])):
        beams[part * SUB : (part + 1) * SUB, :] = jnp.dot(member, white, preferred_element_type=F32).astype(BF16)


def crossing_kernel(keep_right, keep_left, from_even, from_odd, own, group, nearby, scale, *out):
    half = keep_right.shape[0]
    held = out[-1]
    me = lax.axis_index("tchunk")
    even = me % 2 == 0
    got_even = from_even[...].astype(F32)
    got_odd = from_odd[...].astype(F32)
    ahead = keep_right[...] + jnp.where(even, got_even, got_odd)
    behind = keep_left[...] + jnp.where(even, got_odd, got_even)
    spectra = jnp.concatenate([ahead, behind], axis=0)
    station = lax.broadcasted_iota(jnp.int32, group.shape, 1)
    member = members(group[...] + jnp.where(station < half, 0, SUB), 2 * SUB)
    held[: 2 * SUB, :] = own[...]
    for part, white in enumerate(whiten(spectra, nearby[...], scale[...])):
        sums = jnp.dot(member, white, preferred_element_type=F32).astype(BF16)
        for side in range(2):
            row = (2 + 2 * side + part) * SUB
            held[row : row + SUB, :] = sums[side * SUB : (side + 1) * SUB]
    pieces = len(out) - 1
    if pieces > 1:
        width = NBIN // pieces
        for mask in range(pieces):
            start = pl.multiple_of((me ^ mask) * width, width)
            out[mask][...] = held[:, pl.ds(start, width)]
    else:
        out[0][...] = held[...]


def far_first(slabs):
    return [0, *range(slabs - 1, 0, -1)]


def combine_kernel(segments, slabs, *refs):
    pieces, (out, held) = refs[:-2], refs[-2:]
    me = lax.axis_index("tchunk")
    side = 2 * SUB
    order = far_first(slabs)
    for m in range(slabs):
        if len(pieces) == slabs:
            held[me ^ order[m]] = pieces[m][...].astype(F32)
        else:
            held[m] = pieces[0][m].astype(F32)
    for s in range(segments):
        here = held[s // 2, :side, :]
        if s % 2 == 1:
            here = held[s // 2, side : 2 * side, :] + held[s // 2 + 1, 2 * side :, :]
        out[s * side : (s + 1) * side, :] = here.astype(BF16)


def cross_terms(segments, mine, others, out):
    side = 2 * SUB
    real, imag = [], []
    for q in range(SUB):
        real_sum = jnp.zeros((SUB, mine.shape[1]), F32)
        imag_sum = jnp.zeros((SUB, mine.shape[1]), F32)
        for s in range(segments):
            first = s * side
            a, b = mine[first + q : first + q + 1, :], mine[first + SUB + q : first + SUB + q + 1, :]
            c, d = others[first : first + SUB, :], others[first + SUB : first + side, :]
            real_sum += a * c + b * d
            imag_sum += b * c - a * d
        real.append(real_sum * (1.0 / segments))
        imag.append(imag_sum * (1.0 / segments))
    half = SUB * SUB
    out[:, :half] = jnp.transpose(jnp.concatenate(real, axis=0))
    out[:, half:] = jnp.transpose(jnp.concatenate(imag, axis=0))


def near_kernel(segments, own, *refs):
    blocks, (products, mine, others) = refs[:-3], refs[-3:]
    mine[...] = own[...].astype(F32)
    products[0] = jnp.zeros(products.shape[1:], F32)
    for index, block in enumerate(blocks):
        others[...] = block[...].astype(F32)
        cross_terms(segments, mine, others, products.at[index + 1])


def last_kernel(segments, partners, own, block, products, out, mine, others, last, finished):
    home = lax.axis_index("stn")
    count = products.shape[0]
    which = []
    for slot in range(MAXP):
        partner = jnp.max(partners[0:1, slot : slot + 1])
        which.append(jnp.where(partner < 0, 0, partner ^ home))

    def copy(slot, source):
        return pltpu.make_async_copy(source, out.at[slot], finished.at[slot])

    for slot in range(MAXP):
        @pl.when(which[slot] < count)
        def _(slot=slot):
            copy(slot, products.at[jnp.minimum(which[slot], count - 1)]).start()

    mine[...] = own[...].astype(F32)
    others[...] = block[...].astype(F32)
    cross_terms(segments, mine, others, last)
    for slot in range(MAXP):
        @pl.when(which[slot] >= count)
        def _(slot=slot):
            copy(slot, last).start()

    for slot in range(MAXP):
        copy(slot, last).wait()


def cross_kernel(segments, partners, *refs):
    blocks, (out, mine, others, done, finished) = refs[:-5], refs[-5:]
    home = lax.axis_index("stn")
    mine[...] = blocks[0][...].astype(F32)
    copies = []
    for slot in range(MAXP):
        partner = partners[0:1, slot : slot + 1]
        chosen = jnp.zeros(mine.shape, F32)
        for index in range(1, len(blocks)):
            chosen = jnp.where(partner == home ^ index, blocks[index][...].astype(F32), chosen)
        others[...] = chosen
        cross_terms(segments, mine, others, done.at[slot])
        copies.append(pltpu.make_async_copy(done.at[slot], out.at[slot], finished.at[slot]))
        copies[-1].start()
    for copy in copies:
        copy.wait()


def body(raw_data, station_group, partner_blocks):
    stations, samples = raw_data.shape
    slabs = lax.axis_size("tchunk")
    count_blocks = lax.axis_size("stn")
    me, home = lax.axis_index("tchunk"), lax.axis_index("stn")
    blocks = samples // RB
    half = stations // 2
    tapered, table, taper = (jnp.asarray(t) for t in dft_tables())
    nearby, scale = (jnp.asarray(t) for t in smooth_tables())
    group = station_group[None, :]
    shape = jax.ShapeDtypeStruct

    halo = shape((blocks // 2, stations), F32)
    in_hbm = [pltpu.with_memory_space_constraint(a, pltpu.HBM) for a in (raw_data, taper, table)]
    raw, sums, even, odd, taper = call(
        sums_kernel,
        (shape(raw_data.shape, F32), shape((stations, blocks), F32), halo, halo, shape(taper.shape, F32)),
        in_hbm[:2],
        specs=[HBM, HBM],
        scratch_shapes=[pltpu.VMEM((stations, RB), F32), pltpu.SemaphoreType.DMA((4,))],
        flops=10**10,
    )
    even, odd = neighbour_swap(even, odd, True)
    sent = shape((half, 2 * NBIN), BF16)
    kept = shape((half, 2 * NBIN), F32)
    inner = (blocks - 2 * RAMH + 1) * RB
    partial = shape((stations, 2 * NBIN), F32)
    edges = [shape((RAMH - 1, half, 2 * NBIN), F32), shape((RAMH, half, 2 * NBIN), F32)]
    middle, ahead, behind, window, last, first = call(
        middle_kernel,
        (shape((stations, inner), BF16), partial, partial, shape((stations, blocks), F32), *edges),
        (raw, sums, table, taper),
        scratch_shapes=[pltpu.VMEM((stations, inner), BF16), pltpu.VMEM((RAMH, half, RB), BF16)],
        flops=4 * stations * inner * NBIN,
    )
    even, odd, factor = call(
        functools.partial(send_kernel, slabs),
        (sent, sent, shape((stations, blocks), F32)),
        (window, odd, even, ahead, behind, last, first),
        flops=4 * stations * RAMH * NBIN,
    )
    even, odd = neighbour_swap(even, odd, False)
    own, keep_right, keep_left = call(
        own_kernel,
        (shape((2 * SUB, NBIN), BF16), kept, kept),
        (raw, factor, middle, table, tapered, taper, ahead, behind, group, nearby, scale),
        scratch_shapes=[
            pltpu.VMEM((stations, samples), BF16),
            pltpu.VMEM((half, RAMH * RB), BF16),
            pltpu.VMEM((half, (RAMH - 1) * RB), BF16),
        ],
        flops=6 * stations * samples * NBIN,
    )
    direct = slabs <= 8 and slabs & (slabs - 1) == 0 and NBIN // slabs % 128 == 0
    width = NBIN // slabs
    rows = 6 * SUB
    pieces = call(
        crossing_kernel,
        tuple([shape((rows, width), BF16)] * slabs) if direct else (shape((rows, NBIN), BF16),),
        (keep_right, keep_left, even, odd, own, group, nearby, scale),
        scratch_shapes=[pltpu.VMEM((rows, NBIN), BF16)],
        flops=8 * stations * NBIN * NBIN,
        limit=32,
    )
    if direct:
        order = far_first(slabs)[1:]
        received = {m: swapped(pieces[m], "tchunk", m) for m in order}
        received = [pieces[0]] + [received[m] for m in far_first(slabs)[1:]]
    else:
        received = pieces[0].reshape(rows, slabs, width).swapaxes(0, 1)
        received = [lax.all_to_all(received, "tchunk", split_axis=0, concat_axis=0, tiled=True)]
    segments = SEG_DEV * slabs - 1
    mine = call(
        functools.partial(combine_kernel, segments, slabs),
        shape((segments * 2 * SUB, width), BF16),
        received,
        scratch_shapes=[pltpu.VMEM((slabs, rows, width), F32)],
    )
    result = (MAXP, width, 2 * SUB * SUB)
    floats = [pltpu.VMEM(mine.shape, F32)] * 2
    flops = segments * width * SUB * SUB * 8
    if count_blocks == 4:
        across = swapped(mine, "stn", 2)
        beside = swapped(mine, "stn", 1)
        last = swapped(across, "stn", 1)
        products = call(
            functools.partial(near_kernel, segments),
            shape(result, F32),
            (mine, beside, across),
            scratch_shapes=floats,
            flops=2 * flops,
        )
        out = call(
            functools.partial(last_kernel, segments),
            shape(result, F32),
            (partner_blocks, mine, last, products),
            out_specs=HBM,
            scratch_shapes=floats + [pltpu.VMEM(result[1:], F32), pltpu.SemaphoreType.DMA((MAXP,))],
            flops=flops,
        )
    else:
        gathered = lax.all_gather(mine, "stn", axis=0)
        others = [lax.dynamic_index_in_dim(gathered, home ^ m, 0, keepdims=False) for m in range(count_blocks)]
        out = call(
            functools.partial(cross_kernel, segments),
            shape(result, F32),
            (partner_blocks, *others),
            out_specs=HBM,
            scratch_shapes=floats + [pltpu.VMEM(result, F32), pltpu.SemaphoreType.DMA((MAXP,))],
            flops=MAXP * flops,
            limit=32,
        )
    return out[None]


def solution(mesh):
    placed = (P("stn", ("hour", "tchunk")), P("stn"), P("stn", None))
    return jax.shard_map(
        body,
        mesh=mesh,
        in_specs=placed,
        out_specs=P(("hour", "stn"), None, "tchunk", None),
        check_vma=False,
    )
```

```python
import functools
import math

import jax
import jax.numpy as jnp
import ml_dtypes
import numpy as np
from jax import lax
from jax.experimental import pallas as pl
from jax.experimental.pallas import tpu as pltpu
from jax.sharding import PartitionSpec as P

SEG_DEV = 2
SEGLEN = 4096
HOP = 2048
NBIN = 512
RB = 128
RAMH = 10
SMOOTH = 8
SUB = 16
MAXP = 3

EPS_MEAN = 1e-06
LEVEL = 0.05

BF16 = jnp.bfloat16
F32 = jnp.float32
VMEM = pl.BlockSpec(memory_space=pltpu.VMEM)
HBM = pl.BlockSpec(memory_space=pltpu.HBM)
MIB = 1 << 20


def dft_tables():
    sample = np.arange(HOP, dtype=np.int32)
    frequency = np.arange(1, NBIN + 1, dtype=np.int32)
    turn = np.arange(SEGLEN, dtype=np.float64) * (2.0 * math.pi / SEGLEN)
    phases = sample[:, None] * frequency[None, :] % SEGLEN
    matrix = np.concatenate([np.cos(turn)[phases], -np.sin(turn)[phases]], axis=1)
    taper = (0.5 - 0.5 * np.cos(turn)).reshape(2, HOP)
    repeated = np.concatenate([matrix, matrix * np.concatenate([(-1.0) ** frequency] * 2)], axis=0)
    tapered = (taper.reshape(-1, 1) * repeated).astype(np.float32).astype(ml_dtypes.bfloat16)
    matrix = matrix.astype(np.float32).astype(ml_dtypes.bfloat16)
    return tapered, matrix, taper.astype(np.float32)


def smooth_tables():
    bin_index = np.arange(NBIN)
    nearby = np.abs(bin_index[:, None] - bin_index[None, :]) <= SMOOTH
    scale = 1.0 / np.sum(nearby, axis=0, keepdims=True)
    return nearby.astype(ml_dtypes.bfloat16), scale.astype(np.float32)


def neighbour_swap(first, second, outer_first):
    blocks, slabs = lax.axis_size("stn"), lax.axis_size("tchunk")
    inner = [(i, i ^ 1) for i in range(slabs - slabs % 2)]
    outer = [(i, i + 1) for i in range(1, slabs - 1, 2)]
    outer += [(j, i) for i, j in outer]
    pairs = [[(b * slabs + i, b * slabs + j) for b in range(blocks) for i, j in part] for part in (inner, outer)]
    if blocks % 2 == 0 and slabs % 2 == 0:
        pairs[1] += [(b * slabs + i, (b ^ 1) * slabs + i) for b in range(blocks) for i in (0, slabs - 1)]
    sent = {}
    for i in (1, 0) if outer_first else (0, 1):
        sent[i] = lax.ppermute((first, second)[i], ("stn", "tchunk"), pairs[i])
    return sent[0], sent[1]


def swapped(block, axis, mask):
    return lax.ppermute(block, axis, [(i, i ^ mask) for i in range(lax.axis_size(axis))])


def call(kernel, out_shape, operands, specs=None, flops=0, limit=16, **more):
    moved = sum(math.prod(a.shape) * a.dtype.itemsize for a in list(operands) + jax.tree.leaves(out_shape))
    more.setdefault("out_specs", jax.tree.map(lambda _: VMEM, out_shape))
    return pl.pallas_call(
        kernel,
        out_shape=out_shape,
        in_specs=specs or [VMEM] * len(operands),
        compiler_params=pltpu.CompilerParams(vmem_limit_bytes=limit * MIB),
        cost_estimate=pl.CostEstimate(flops=flops, bytes_accessed=moved, transcendentals=0),
        **more,
    )(*operands)


def sums_kernel(source, taper_source, raw, sums, to_even, to_odd, taper, held, arrived):
    chunks = arrived.shape[0] - 1
    stations, samples = raw.shape
    blocks = samples // RB
    ends = [stations * n // 9 // 8 * 8 for n in (0, 3, 6, 9)]
    copies = []
    for step in range(chunks):
        rows = ends[step + 1] - ends[step]
        here = pl.ds(ends[step], rows)
        copies.append(pltpu.make_async_copy(source.at[here], raw.at[here], arrived.at[step]))
        copies[-1].start()
    copies.append(pltpu.make_async_copy(taper_source, taper, arrived.at[chunks]))
    copies[-1].start()
    for step in range(chunks):
        copies[step].wait()
        rows = ends[step + 1] - ends[step]
        here = pl.ds(ends[step], rows)
        lane = lax.broadcasted_iota(jnp.int32, (rows, RB), 1)
        total = jnp.zeros((rows, RB), F32)
        for b in range(blocks):
            amount = jnp.sum(jnp.abs(raw[here, b * RB : (b + 1) * RB]), axis=1, keepdims=True)
            total = jnp.where(lane == b, amount, total)
        held[here, :] = total
    whole = held[...]
    sums[...] = whole[:, :blocks]
    flipped = jnp.transpose(whole)
    head = flipped[: blocks // 2]
    tail = flipped[blocks // 2 : blocks]
    even = lax.axis_index("tchunk") % 2 == 0
    to_even[...] = jnp.where(even, tail, head)
    to_odd[...] = jnp.where(even, head, tail)
    copies[-1].wait()


def split_dot(left, right, axis):
    high = left.astype(BF16)
    rest = left - high.astype(F32)
    middle = rest.astype(BF16)
    low = (rest - middle.astype(F32)).astype(BF16)
    parts = jnp.concatenate([high, middle, low], axis=axis)
    return lax.dot_general(
        parts, jnp.concatenate([right] * 3, axis=0), (((axis,), (0,)), ((), ())), preferred_element_type=F32
    )


def band(rows, blocks, first):
    source = lax.broadcasted_iota(jnp.int32, (rows, blocks), 0) + first
    target = lax.broadcasted_iota(jnp.int32, (rows, blocks), 1)
    return ((source >= target - RAMH) & (source < target + RAMH)).astype(BF16)


def alternating():
    column = lax.broadcasted_iota(jnp.int32, (1, 2 * NBIN), 1)
    return jnp.where(column % 2 == 0, -1.0, 1.0)


def windowed_blocks(raw, factor, taper, rows, some, normal, windowed):
    for place, b in enumerate(some):
        here = pl.ds(place * RB, RB)
        scaled = (raw[rows, b * RB : (b + 1) * RB] * factor[rows, b : b + 1]).astype(BF16)
        if normal is not None:
            normal[:, here] = scaled
        hop, inside = divmod(b * RB, HOP)
        weight = taper[1 - hop : 2 - hop, inside : inside + RB]
        windowed[:, here] = (scaled.astype(F32) * weight).astype(BF16)


def middle_kernel(raw, sums, table, taper, normal, ahead, behind, window, last, first, windowed, bare):
    blocks = sums.shape[1]
    half = raw.shape[0] // 2
    for source, rows, some, out in (
        (raw, slice(half, None), range(blocks - RAMH + 1, blocks), last),
        (raw, slice(0, half), range(RAMH), first),
    ):
        for place, b in enumerate(some):
            hop, inside = divmod(b * RB, HOP)
            weight = taper[1 - hop : 2 - hop, inside : inside + RB]
            bare[place] = (source[rows, b * RB : (b + 1) * RB] * weight).astype(BF16)
            out[place] = jnp.dot(bare[place], table[inside : inside + RB, :], preferred_element_type=F32)

    window[...] = split_dot(sums[...], band(blocks, blocks, 0), 1)
    factor = 1.0 / (window[...] * (1.0 / (2 * RAMH * RB)) + EPS_MEAN)
    windowed_blocks(raw, factor, taper, slice(None), range(RAMH, blocks - RAMH + 1), normal, windowed)
    split = HOP - RAMH * RB
    rest = windowed.shape[1] - split
    ahead[...] = jnp.dot(windowed[:, split:], table[:rest, :], preferred_element_type=F32)
    behind[...] = jnp.dot(windowed[:, :split], table[HOP - split :, :], preferred_element_type=F32)


def send_kernel(slabs, window, from_odd, from_even, ahead, behind, last, first, to_even, to_odd, factor):
    stations, blocks = window.shape
    half_blocks = from_even.shape[0]
    half = stations // 2
    me = lax.axis_index("tchunk")
    even = me % 2 == 0
    left = jnp.where(even, from_odd[...], from_even[...])
    right = jnp.where(even, from_even[...], from_odd[...])
    left = jnp.where(me > 0, left, 0.0)
    right = jnp.where(me < slabs - 1, right, 0.0)
    near = jnp.concatenate([left, right], axis=0)
    bands = jnp.concatenate([band(half_blocks, blocks, -half_blocks), band(half_blocks, blocks, blocks)], axis=0)
    total = window[...] + split_dot(near, bands, 0)
    block = lax.broadcasted_iota(jnp.int32, (stations, blocks), 1) + me * blocks
    counted = jnp.minimum(block + RAMH, slabs * blocks) - jnp.maximum(block - RAMH, 0)
    factor[...] = 1.0 / (total / (RB * counted.astype(F32)) + EPS_MEAN)
    sign = alternating()

    def weighted(base, products, start, first):
        sums = []
        for row in range(0, half, 8):
            here = slice(start + row, start + row + 8)
            total = base[here, :]
            for place in range(products.shape[0]):
                b = first + place
                total += factor[here, b : b + 1] * products[place, row : row + 8, :]
            sums.append(total)
        return jnp.concatenate(sums, axis=0)

    def fill(to_right, to_left):
        to_right[...] = weighted(ahead, last, half, blocks - RAMH + 1).astype(BF16)
        to_left[...] = (weighted(behind, first, 0, 0) * sign).astype(BF16)

    @pl.when(even)
    def _():
        fill(to_even, to_odd)

    @pl.when(jnp.logical_not(even))
    def _():
        fill(to_odd, to_even)


def whiten(spectra, nearby, scale):
    rows = spectra.shape[0]
    real_part = spectra[:, :NBIN]
    imag_part = spectra[:, NBIN:]
    powers = real_part * real_part + imag_part * imag_part
    high = powers.astype(BF16)
    low = (powers - high.astype(F32)).astype(BF16)
    both = jnp.dot(jnp.concatenate([high, low], axis=0), nearby, preferred_element_type=F32)
    smooth = both[:rows] + both[rows:]
    floor_level = jnp.sum(powers, axis=1, keepdims=True) * (1.0 / NBIN) + 1e-06
    inverse = lax.rsqrt(smooth * scale + LEVEL * floor_level)
    return (real_part * inverse).astype(BF16), (imag_part * inverse).astype(BF16)


def members(group, count):
    shape = (count, group.shape[1])
    return (lax.broadcasted_iota(jnp.int32, shape, 0) == group).astype(BF16)


def own_kernel(
    raw, factor, middle, table, tapered, taper, ahead, behind, group, nearby, scale,
    beams, keep_right, keep_left, normal, first, last,
):
    stations, blocks = factor.shape
    half = stations // 2
    windowed_blocks(raw, factor, taper, slice(0, half), range(blocks - RAMH + 1, blocks), None, last)
    windowed_blocks(raw, factor, taper, slice(half, stations), range(RAMH), None, first)
    part = jnp.dot(last[...], table[HOP - last.shape[1] :, :], preferred_element_type=F32)
    keep_right[...] = part + ahead[:half]
    part = jnp.dot(first[...], table[: first.shape[1], :], preferred_element_type=F32)
    keep_left[...] = (part + behind[half:]) * alternating()

    for b in [*range(RAMH), *range(blocks - RAMH + 1, blocks)]:
        here = pl.ds(b * RB, RB)
        normal[:, here] = (raw[:, here] * factor[:, b : b + 1]).astype(BF16)
    normal[:, RAMH * RB : RAMH * RB + middle.shape[1]] = middle[...]
    spectra = jnp.dot(normal[...], tapered[...], preferred_element_type=F32)
    member = members(group[...], SUB)
    for part, white in enumerate(whiten(spectra, nearby[...], scale[...])):
        beams[part * SUB : (part + 1) * SUB, :] = jnp.dot(member, white, preferred_element_type=F32).astype(BF16)


def crossing_kernel(keep_right, keep_left, from_even, from_odd, own, group, nearby, scale, *out):
    half = keep_right.shape[0]
    held = out[-1]
    me = lax.axis_index("tchunk")
    even = me % 2 == 0
    got_even, got_odd = from_even[...], from_odd[...]
    ahead = keep_right[...] + jnp.where(even, got_even, got_odd).astype(F32)
    behind = keep_left[...] + jnp.where(even, got_odd, got_even).astype(F32)
    spectra = jnp.concatenate([ahead, behind], axis=0)
    station = lax.broadcasted_iota(jnp.int32, group.shape, 1)
    member = members(group[...] + jnp.where(station < half, 0, SUB), 2 * SUB)
    held[: 2 * SUB, :] = own[...]
    for part, white in enumerate(whiten(spectra, nearby[...], scale[...])):
        sums = jnp.dot(member, white, preferred_element_type=F32).astype(BF16)
        for side in range(2):
            row = (2 + 2 * side + part) * SUB
            held[row : row + SUB, :] = sums[side * SUB : (side + 1) * SUB]
    pieces = len(out) - 1
    if pieces > 1:
        width = NBIN // pieces
        for mask in range(pieces):
            start = pl.multiple_of((me ^ mask) * width, width)
            out[mask][...] = held[:, pl.ds(start, width)]
    else:
        out[0][...] = held[...]


def far_first(slabs):
    return [0, *range(slabs - 1, 0, -1)]


def combine_kernel(segments, slabs, *refs):
    pieces, (out, held) = refs[:-2], refs[-2:]
    me = lax.axis_index("tchunk")
    side = 2 * SUB
    order = far_first(slabs)
    for m in range(slabs):
        if len(pieces) == slabs:
            held[me ^ order[m]] = pieces[m][...].astype(F32)
        else:
            held[m] = pieces[0][m].astype(F32)
    for s in range(segments):
        here = held[s // 2, :side, :]
        if s % 2 == 1:
            here = held[s // 2, side : 2 * side, :] + held[s // 2 + 1, 2 * side :, :]
        out[s * side : (s + 1) * side, :] = here.astype(BF16)


def cross_terms(segments, mine, others, out):
    side = 2 * SUB
    real, imag = [], []
    for q in range(SUB):
        real_sum = jnp.zeros((SUB, mine.shape[1]), F32)
        imag_sum = jnp.zeros((SUB, mine.shape[1]), F32)
        for s in range(segments):
            first = s * side
            a, b = mine[first + q : first + q + 1, :], mine[first + SUB + q : first + SUB + q + 1, :]
            c, d = others[first : first + SUB, :], others[first + SUB : first + side, :]
            real_sum += a * c + b * d
            imag_sum += b * c - a * d
        real.append(real_sum * (1.0 / segments))
        imag.append(imag_sum * (1.0 / segments))
    half = SUB * SUB
    out[:, :half] = jnp.transpose(jnp.concatenate(real, axis=0))
    out[:, half:] = jnp.transpose(jnp.concatenate(imag, axis=0))


def near_kernel(segments, own, *refs):
    blocks, (products, mine, others) = refs[:-3], refs[-3:]
    mine[...] = own[...].astype(F32)
    products[0] = jnp.zeros(products.shape[1:], F32)
    for index, block in enumerate(blocks):
        others[...] = block[...].astype(F32)
        cross_terms(segments, mine, others, products.at[index + 1])


def last_kernel(segments, partners, own, block, products, out, mine, others, last, finished):
    home = lax.axis_index("stn")
    count = products.shape[0]
    which = []
    for slot in range(MAXP):
        partner = jnp.max(partners[0:1, slot : slot + 1])
        which.append(jnp.where(partner < 0, 0, partner ^ home))

    def copy(slot, source):
        return pltpu.make_async_copy(source, out.at[slot], finished.at[slot])

    for slot in range(MAXP):
        @pl.when(which[slot] < count)
        def _(slot=slot):
            copy(slot, products.at[jnp.minimum(which[slot], count - 1)]).start()

    mine[...] = own[...].astype(F32)
    others[...] = block[...].astype(F32)
    cross_terms(segments, mine, others, last)
    for slot in range(MAXP):
        @pl.when(which[slot] >= count)
        def _(slot=slot):
            copy(slot, last).start()

    for slot in range(MAXP):
        copy(slot, last).wait()


def cross_kernel(segments, partners, *refs):
    blocks, (out, mine, others, done, finished) = refs[:-5], refs[-5:]
    home = lax.axis_index("stn")
    mine[...] = blocks[0][...].astype(F32)
    copies = []
    for slot in range(MAXP):
        partner = partners[0:1, slot : slot + 1]
        chosen = jnp.zeros(mine.shape, F32)
        for index in range(1, len(blocks)):
            chosen = jnp.where(partner == home ^ index, blocks[index][...].astype(F32), chosen)
        others[...] = chosen
        cross_terms(segments, mine, others, done.at[slot])
        copies.append(pltpu.make_async_copy(done.at[slot], out.at[slot], finished.at[slot]))
        copies[-1].start()
    for copy in copies:
        copy.wait()


def body(raw_data, station_group, partner_blocks):
    stations, samples = raw_data.shape
    slabs = lax.axis_size("tchunk")
    count_blocks = lax.axis_size("stn")
    me, home = lax.axis_index("tchunk"), lax.axis_index("stn")
    blocks = samples // RB
    half = stations // 2
    tapered, table, taper = (jnp.asarray(t) for t in dft_tables())
    nearby, scale = (jnp.asarray(t) for t in smooth_tables())
    group = station_group[None, :]
    shape = jax.ShapeDtypeStruct

    halo = shape((blocks // 2, stations), F32)
    in_hbm = [pltpu.with_memory_space_constraint(a, pltpu.HBM) for a in (raw_data, taper, table)]
    raw, sums, even, odd, taper = call(
        sums_kernel,
        (shape(raw_data.shape, F32), shape((stations, blocks), F32), halo, halo, shape(taper.shape, F32)),
        in_hbm[:2],
        specs=[HBM, HBM],
        scratch_shapes=[pltpu.VMEM((stations, RB), F32), pltpu.SemaphoreType.DMA((4,))],
        flops=10**10,
    )
    even, odd = neighbour_swap(even, odd, True)
    sent = shape((half, 2 * NBIN), BF16)
    kept = shape((half, 2 * NBIN), F32)
    inner = (blocks - 2 * RAMH + 1) * RB
    partial = shape((stations, 2 * NBIN), F32)
    edges = [shape((RAMH - 1, half, 2 * NBIN), F32), shape((RAMH, half, 2 * NBIN), F32)]
    middle, ahead, behind, window, last, first = call(
        middle_kernel,
        (shape((stations, inner), BF16), partial, partial, shape((stations, blocks), F32), *edges),
        (raw, sums, table, taper),
        scratch_shapes=[pltpu.VMEM((stations, inner), BF16), pltpu.VMEM((RAMH, half, RB), BF16)],
        flops=4 * stations * inner * NBIN,
    )
    even, odd, factor = call(
        functools.partial(send_kernel, slabs),
        (sent, sent, shape((stations, blocks), F32)),
        (window, odd, even, ahead, behind, last, first),
        flops=4 * stations * RAMH * NBIN,
    )
    even, odd = neighbour_swap(even, odd, False)
    own, keep_right, keep_left = call(
        own_kernel,
        (shape((2 * SUB, NBIN), BF16), kept, kept),
        (raw, factor, middle, table, tapered, taper, ahead, behind, group, nearby, scale),
        scratch_shapes=[
            pltpu.VMEM((stations, samples), BF16),
            pltpu.VMEM((half, RAMH * RB), BF16),
            pltpu.VMEM((half, (RAMH - 1) * RB), BF16),
        ],
        flops=6 * stations * samples * NBIN,
    )
    direct = slabs <= 8 and slabs & (slabs - 1) == 0 and NBIN // slabs % 128 == 0
    width = NBIN // slabs
    rows = 6 * SUB
    pieces = call(
        crossing_kernel,
        tuple([shape((rows, width), BF16)] * slabs) if direct else (shape((rows, NBIN), BF16),),
        (keep_right, keep_left, even, odd, own, group, nearby, scale),
        scratch_shapes=[pltpu.VMEM((rows, NBIN), BF16)],
        flops=8 * stations * NBIN * NBIN,
        limit=32,
    )
    if direct:
        order = far_first(slabs)[1:]
        received = {m: swapped(pieces[m], "tchunk", m) for m in order}
        received = [pieces[0]] + [received[m] for m in far_first(slabs)[1:]]
    else:
        received = pieces[0].reshape(rows, slabs, width).swapaxes(0, 1)
        received = [lax.all_to_all(received, "tchunk", split_axis=0, concat_axis=0, tiled=True)]
    segments = SEG_DEV * slabs - 1
    mine = call(
        functools.partial(combine_kernel, segments, slabs),
        shape((segments * 2 * SUB, width), BF16),
        received,
        scratch_shapes=[pltpu.VMEM((slabs, rows, width), F32)],
    )
    result = (MAXP, width, 2 * SUB * SUB)
    floats = [pltpu.VMEM(mine.shape, F32)] * 2
    flops = segments * width * SUB * SUB * 8
    if count_blocks == 4:
        across = swapped(mine, "stn", 2)
        beside = swapped(mine, "stn", 1)
        last = swapped(across, "stn", 1)
        products = call(
            functools.partial(near_kernel, segments),
            shape(result, F32),
            (mine, beside, across),
            scratch_shapes=floats,
            flops=2 * flops,
        )
        out = call(
            functools.partial(last_kernel, segments),
            shape(result, F32),
            (partner_blocks, mine, last, products),
            out_specs=HBM,
            scratch_shapes=floats + [pltpu.VMEM(result[1:], F32), pltpu.SemaphoreType.DMA((MAXP,))],
            flops=flops,
        )
    else:
        gathered = lax.all_gather(mine, "stn", axis=0)
        others = [lax.dynamic_index_in_dim(gathered, home ^ m, 0, keepdims=False) for m in range(count_blocks)]
        out = call(
            functools.partial(cross_kernel, segments),
            shape(result, F32),
            (partner_blocks, *others),
            out_specs=HBM,
            scratch_shapes=floats + [pltpu.VMEM(result, F32), pltpu.SemaphoreType.DMA((MAXP,))],
            flops=MAXP * flops,
            limit=32,
        )
    return out[None]


def solution(mesh):
    placed = (P("stn", ("hour", "tchunk")), P("stn"), P("stn", None))
    return jax.shard_map(
        body,
        mesh=mesh,
        in_specs=placed,
        out_specs=P(("hour", "stn"), None, "tchunk", None),
        check_vma=False,
    )
```

```python
import functools
import math

import jax
import jax.numpy as jnp
import ml_dtypes
import numpy as np
from jax import lax
from jax.experimental import pallas as pl
from jax.experimental.pallas import tpu as pltpu
from jax.sharding import PartitionSpec as P

SEG_DEV = 2
SEGLEN = 4096
HOP = 2048
NBIN = 512
RB = 128
RAMH = 10
SMOOTH = 8
SUB = 16
MAXP = 3

EPS_MEAN = 1e-06
LEVEL = 0.05

BF16 = jnp.bfloat16
F32 = jnp.float32
VMEM = pl.BlockSpec(memory_space=pltpu.VMEM)
HBM = pl.BlockSpec(memory_space=pltpu.HBM)
MIB = 1 << 20


def dft_tables():
    sample = np.arange(HOP, dtype=np.int32)
    frequency = np.arange(1, NBIN + 1, dtype=np.int32)
    turn = np.arange(SEGLEN, dtype=np.float64) * (2.0 * math.pi / SEGLEN)
    phases = sample[:, None] * frequency[None, :] % SEGLEN
    matrix = np.concatenate([np.cos(turn)[phases], -np.sin(turn)[phases]], axis=1)
    taper = (0.5 - 0.5 * np.cos(turn)).reshape(2, HOP)
    repeated = np.concatenate([matrix, matrix * np.concatenate([(-1.0) ** frequency] * 2)], axis=0)
    tapered = (taper.reshape(-1, 1) * repeated).astype(np.float32).astype(ml_dtypes.bfloat16)
    matrix = matrix.astype(np.float32).astype(ml_dtypes.bfloat16)
    return tapered, matrix, taper.astype(np.float32)


def smooth_tables():
    bin_index = np.arange(NBIN)
    nearby = np.abs(bin_index[:, None] - bin_index[None, :]) <= SMOOTH
    scale = 1.0 / np.sum(nearby, axis=0, keepdims=True)
    return nearby.astype(ml_dtypes.bfloat16), scale.astype(np.float32)


def neighbour_swap(first, second, outer_first):
    blocks, slabs = lax.axis_size("stn"), lax.axis_size("tchunk")
    inner = [(i, i ^ 1) for i in range(slabs - slabs % 2)]
    outer = [(i, i + 1) for i in range(1, slabs - 1, 2)]
    outer += [(j, i) for i, j in outer]
    pairs = [[(b * slabs + i, b * slabs + j) for b in range(blocks) for i, j in part] for part in (inner, outer)]
    if blocks % 2 == 0 and slabs % 2 == 0:
        pairs[1] += [(b * slabs + i, (b ^ 1) * slabs + i) for b in range(blocks) for i in (0, slabs - 1)]
    sent = {}
    for i in (1, 0) if outer_first else (0, 1):
        sent[i] = lax.ppermute((first, second)[i], ("stn", "tchunk"), pairs[i])
    return sent[0], sent[1]


def swapped(block, axis, mask):
    return lax.ppermute(block, axis, [(i, i ^ mask) for i in range(lax.axis_size(axis))])


def call(kernel, out_shape, operands, specs=None, flops=0, limit=16, **more):
    moved = sum(math.prod(a.shape) * a.dtype.itemsize for a in list(operands) + jax.tree.leaves(out_shape))
    more.setdefault("out_specs", jax.tree.map(lambda _: VMEM, out_shape))
    return pl.pallas_call(
        kernel,
        out_shape=out_shape,
        in_specs=specs or [VMEM] * len(operands),
        compiler_params=pltpu.CompilerParams(vmem_limit_bytes=limit * MIB),
        cost_estimate=pl.CostEstimate(flops=flops, bytes_accessed=moved, transcendentals=0),
        **more,
    )(*operands)


def sums_kernel(source, taper_source, raw, sums, to_even, to_odd, taper, held, arrived):
    chunks = arrived.shape[0] - 1
    stations, samples = raw.shape
    blocks = samples // RB
    ends = [stations * n // 9 // 8 * 8 for n in (0, 3, 6, 9)]
    copies = []
    for step in range(chunks):
        rows = ends[step + 1] - ends[step]
        here = pl.ds(ends[step], rows)
        copies.append(pltpu.make_async_copy(source.at[here], raw.at[here], arrived.at[step]))
        copies[-1].start()
    copies.append(pltpu.make_async_copy(taper_source, taper, arrived.at[chunks]))
    copies[-1].start()
    for step in range(chunks):
        copies[step].wait()
        rows = ends[step + 1] - ends[step]
        here = pl.ds(ends[step], rows)
        lane = lax.broadcasted_iota(jnp.int32, (rows, RB), 1)
        total = jnp.zeros((rows, RB), F32)
        for b in range(blocks):
            amount = jnp.sum(jnp.abs(raw[here, b * RB : (b + 1) * RB]), axis=1, keepdims=True)
            total = jnp.where(lane == b, amount, total)
        held[here, :] = total
    whole = held[...]
    sums[...] = whole[:, :blocks]
    flipped = jnp.transpose(whole)
    head = flipped[: blocks // 2]
    tail = flipped[blocks // 2 : blocks]
    even = lax.axis_index("tchunk") % 2 == 0
    to_even[...] = jnp.where(even, tail, head)
    to_odd[...] = jnp.where(even, head, tail)
    copies[-1].wait()


def split_dot(left, right, axis):
    high = left.astype(BF16)
    rest = left - high.astype(F32)
    middle = rest.astype(BF16)
    low = (rest - middle.astype(F32)).astype(BF16)
    parts = jnp.concatenate([high, middle, low], axis=axis)
    return lax.dot_general(
        parts, jnp.concatenate([right] * 3, axis=0), (((axis,), (0,)), ((), ())), preferred_element_type=F32
    )


def band(rows, blocks, first):
    source = lax.broadcasted_iota(jnp.int32, (rows, blocks), 0) + first
    target = lax.broadcasted_iota(jnp.int32, (rows, blocks), 1)
    return ((source >= target - RAMH) & (source < target + RAMH)).astype(BF16)


def alternating():
    column = lax.broadcasted_iota(jnp.int32, (1, 2 * NBIN), 1)
    return jnp.where(column % 2 == 0, -1.0, 1.0)


def windowed_blocks(raw, factor, taper, rows, some, normal, windowed):
    for place, b in enumerate(some):
        here = pl.ds(place * RB, RB)
        scaled = (raw[rows, b * RB : (b + 1) * RB] * factor[rows, b : b + 1]).astype(BF16)
        if normal is not None:
            normal[:, here] = scaled
        hop, inside = divmod(b * RB, HOP)
        weight = taper[1 - hop : 2 - hop, inside : inside + RB]
        windowed[:, here] = (scaled.astype(F32) * weight).astype(BF16)


def middle_kernel(raw, sums, table, taper, normal, ahead, behind, window, last, first, windowed, bare):
    blocks = sums.shape[1]
    half = raw.shape[0] // 2
    for source, rows, some, out in (
        (raw, slice(half, None), range(blocks - RAMH + 1, blocks), last),
        (raw, slice(0, half), range(RAMH), first),
    ):
        for place, b in enumerate(some):
            hop, inside = divmod(b * RB, HOP)
            weight = taper[1 - hop : 2 - hop, inside : inside + RB]
            bare[place] = (source[rows, b * RB : (b + 1) * RB] * weight).astype(BF16)
            out[place] = jnp.dot(bare[place], table[inside : inside + RB, :], preferred_element_type=F32)

    window[...] = split_dot(sums[...], band(blocks, blocks, 0), 1)
    factor = 1.0 / (window[...] * (1.0 / (2 * RAMH * RB)) + EPS_MEAN)
    windowed_blocks(raw, factor, taper, slice(None), range(RAMH, blocks - RAMH + 1), normal, windowed)
    split = HOP - RAMH * RB
    rest = windowed.shape[1] - split
    ahead[...] = jnp.dot(windowed[:, split:], table[:rest, :], preferred_element_type=F32)
    behind[...] = jnp.dot(windowed[:, :split], table[HOP - split :, :], preferred_element_type=F32)


def send_kernel(slabs, window, from_even, from_odd, ahead, behind, last, first, to_even, to_odd, factor):
    stations, blocks = window.shape
    half_blocks = from_even.shape[0]
    half = stations // 2
    me = lax.axis_index("tchunk")
    even = me % 2 == 0
    left = jnp.where(even, from_odd[...], from_even[...])
    right = jnp.where(even, from_even[...], from_odd[...])
    left = jnp.where(me > 0, left, 0.0)
    right = jnp.where(me < slabs - 1, right, 0.0)
    near = jnp.concatenate([left, right], axis=0)
    bands = jnp.concatenate([band(half_blocks, blocks, -half_blocks), band(half_blocks, blocks, blocks)], axis=0)
    total = window[...] + split_dot(near, bands, 0)
    block = lax.broadcasted_iota(jnp.int32, (stations, blocks), 1) + me * blocks
    counted = jnp.minimum(block + RAMH, slabs * blocks) - jnp.maximum(block - RAMH, 0)
    factor[...] = 1.0 / (total / (RB * counted.astype(F32)) + EPS_MEAN)
    sign = alternating()

    def weighted(base, products, start, first):
        sums = []
        for row in range(0, half, 8):
            here = slice(start + row, start + row + 8)
            total = base[here, :]
            for place in range(products.shape[0]):
                b = first + place
                total += factor[here, b : b + 1] * products[place, row : row + 8, :]
            sums.append(total)
        return jnp.concatenate(sums, axis=0)

    def fill(to_right, to_left):
        to_right[...] = weighted(ahead, last, half, blocks - RAMH + 1).astype(BF16)
        to_left[...] = (weighted(behind, first, 0, 0) * sign).astype(BF16)

    @pl.when(even)
    def _():
        fill(to_even, to_odd)

    @pl.when(jnp.logical_not(even))
    def _():
        fill(to_odd, to_even)


def whiten(spectra, nearby, scale):
    rows = spectra.shape[0]
    real_part = spectra[:, :NBIN]
    imag_part = spectra[:, NBIN:]
    powers = real_part * real_part + imag_part * imag_part
    high = powers.astype(BF16)
    low = (powers - high.astype(F32)).astype(BF16)
    both = jnp.dot(jnp.concatenate([high, low], axis=0), nearby, preferred_element_type=F32)
    smooth = both[:rows] + both[rows:]
    floor_level = jnp.sum(powers, axis=1, keepdims=True) * (1.0 / NBIN) + 1e-06
    inverse = lax.rsqrt(smooth * scale + LEVEL * floor_level)
    return (real_part * inverse).astype(BF16), (imag_part * inverse).astype(BF16)


def members(group, count):
    shape = (count, group.shape[1])
    return (lax.broadcasted_iota(jnp.int32, shape, 0) == group).astype(BF16)


def own_kernel(
    raw, factor, middle, table, tapered, taper, ahead, behind, group, nearby, scale,
    beams, keep_right, keep_left, normal, first, last,
):
    stations, blocks = factor.shape
    half = stations // 2
    windowed_blocks(raw, factor, taper, slice(0, half), range(blocks - RAMH + 1, blocks), None, last)
    windowed_blocks(raw, factor, taper, slice(half, stations), range(RAMH), None, first)
    part = jnp.dot(last[...], table[HOP - last.shape[1] :, :], preferred_element_type=F32)
    keep_right[...] = part + ahead[:half]
    part = jnp.dot(first[...], table[: first.shape[1], :], preferred_element_type=F32)
    keep_left[...] = (part + behind[half:]) * alternating()

    for b in [*range(RAMH), *range(blocks - RAMH + 1, blocks)]:
        here = pl.ds(b * RB, RB)
        normal[:, here] = (raw[:, here] * factor[:, b : b + 1]).astype(BF16)
    normal[:, RAMH * RB : RAMH * RB + middle.shape[1]] = middle[...]
    spectra = jnp.dot(normal[...], tapered[...], preferred_element_type=F32)
    member = members(group[...], SUB)
    for part, white in enumerate(whiten(spectra, nearby[...], scale[...])):
        beams[part * SUB : (part + 1) * SUB, :] = jnp.dot(member, white, preferred_element_type=F32).astype(BF16)


def crossing_kernel(keep_right, keep_left, from_even, from_odd, own, group, nearby, scale, *out):
    half = keep_right.shape[0]
    held = out[-1]
    me = lax.axis_index("tchunk")
    even = me % 2 == 0
    got_even, got_odd = from_even[...], from_odd[...]
    ahead = keep_right[...] + jnp.where(even, got_even, got_odd).astype(F32)
    behind = keep_left[...] + jnp.where(even, got_odd, got_even).astype(F32)
    spectra = jnp.concatenate([ahead, behind], axis=0)
    station = lax.broadcasted_iota(jnp.int32, group.shape, 1)
    member = members(group[...] + jnp.where(station < half, 0, SUB), 2 * SUB)
    held[: 2 * SUB, :] = own[...]
    for part, white in enumerate(whiten(spectra, nearby[...], scale[...])):
        sums = jnp.dot(member, white, preferred_element_type=F32).astype(BF16)
        for side in range(2):
            row = (2 + 2 * side + part) * SUB
            held[row : row + SUB, :] = sums[side * SUB : (side + 1) * SUB]
    pieces = len(out) - 1
    if pieces > 1:
        width = NBIN // pieces
        for mask in range(pieces):
            start = pl.multiple_of((me ^ mask) * width, width)
            out[mask][...] = held[:, pl.ds(start, width)]
    else:
        out[0][...] = held[...]


def far_first(slabs):
    return [0, *range(slabs - 1, 0, -1)]


def combine_kernel(segments, slabs, *refs):
    pieces, (out, held) = refs[:-2], refs[-2:]
    me = lax.axis_index("tchunk")
    side = 2 * SUB
    order = far_first(slabs)
    for m in range(slabs):
        if len(pieces) == slabs:
            held[me ^ order[m]] = pieces[m][...].astype(F32)
        else:
            held[m] = pieces[0][m].astype(F32)
    for s in range(segments):
        here = held[s // 2, :side, :]
        if s % 2 == 1:
            here = held[s // 2, side : 2 * side, :] + held[s // 2 + 1, 2 * side :, :]
        out[s * side : (s + 1) * side, :] = here.astype(BF16)


def cross_terms(segments, mine, others, out):
    side = 2 * SUB
    real, imag = [], []
    for q in range(SUB):
        real_sum = jnp.zeros((SUB, mine.shape[1]), F32)
        imag_sum = jnp.zeros((SUB, mine.shape[1]), F32)
        for s in range(segments):
            first = s * side
            a, b = mine[first + q : first + q + 1, :], mine[first + SUB + q : first + SUB + q + 1, :]
            c, d = others[first : first + SUB, :], others[first + SUB : first + side, :]
            real_sum += a * c + b * d
            imag_sum += b * c - a * d
        real.append(real_sum * (1.0 / segments))
        imag.append(imag_sum * (1.0 / segments))
    half = SUB * SUB
    out[:, :half] = jnp.transpose(jnp.concatenate(real, axis=0))
    out[:, half:] = jnp.transpose(jnp.concatenate(imag, axis=0))


def near_kernel(segments, own, *refs):
    blocks, (products, mine, others) = refs[:-3], refs[-3:]
    mine[...] = own[...].astype(F32)
    products[0] = jnp.zeros(products.shape[1:], F32)
    for index, block in enumerate(blocks):
        others[...] = block[...].astype(F32)
        cross_terms(segments, mine, others, products.at[index + 1])


def last_kernel(segments, partners, own, block, products, out, mine, others, last, finished):
    home = lax.axis_index("stn")
    count = products.shape[0]
    which = []
    for slot in range(MAXP):
        partner = jnp.max(partners[0:1, slot : slot + 1])
        which.append(jnp.where(partner < 0, 0, partner ^ home))

    def copy(slot, source):
        return pltpu.make_async_copy(source, out.at[slot], finished.at[slot])

    for slot in range(MAXP):
        @pl.when(which[slot] < count)
        def _(slot=slot):
            copy(slot, products.at[jnp.minimum(which[slot], count - 1)]).start()

    mine[...] = own[...].astype(F32)
    others[...] = block[...].astype(F32)
    cross_terms(segments, mine, others, last)
    for slot in range(MAXP):
        @pl.when(which[slot] >= count)
        def _(slot=slot):
            copy(slot, last).start()

    for slot in range(MAXP):
        copy(slot, last).wait()


def cross_kernel(segments, partners, *refs):
    blocks, (out, mine, others, done, finished) = refs[:-5], refs[-5:]
    home = lax.axis_index("stn")
    mine[...] = blocks[0][...].astype(F32)
    copies = []
    for slot in range(MAXP):
        partner = partners[0:1, slot : slot + 1]
        chosen = jnp.zeros(mine.shape, F32)
        for index in range(1, len(blocks)):
            chosen = jnp.where(partner == home ^ index, blocks[index][...].astype(F32), chosen)
        others[...] = chosen
        cross_terms(segments, mine, others, done.at[slot])
        copies.append(pltpu.make_async_copy(done.at[slot], out.at[slot], finished.at[slot]))
        copies[-1].start()
    for copy in copies:
        copy.wait()


def body(raw_data, station_group, partner_blocks):
    stations, samples = raw_data.shape
    slabs = lax.axis_size("tchunk")
    count_blocks = lax.axis_size("stn")
    me, home = lax.axis_index("tchunk"), lax.axis_index("stn")
    blocks = samples // RB
    half = stations // 2
    tapered, table, taper = (jnp.asarray(t) for t in dft_tables())
    nearby, scale = (jnp.asarray(t) for t in smooth_tables())
    group = station_group[None, :]
    shape = jax.ShapeDtypeStruct

    halo = shape((blocks // 2, stations), F32)
    in_hbm = [pltpu.with_memory_space_constraint(a, pltpu.HBM) for a in (raw_data, taper, table)]
    raw, sums, even, odd, taper = call(
        sums_kernel,
        (shape(raw_data.shape, F32), shape((stations, blocks), F32), halo, halo, shape(taper.shape, F32)),
        in_hbm[:2],
        specs=[HBM, HBM],
        scratch_shapes=[pltpu.VMEM((stations, RB), F32), pltpu.SemaphoreType.DMA((4,))],
        flops=10**10,
    )
    even, odd = neighbour_swap(even, odd, True)
    sent = shape((half, 2 * NBIN), BF16)
    kept = shape((half, 2 * NBIN), F32)
    inner = (blocks - 2 * RAMH + 1) * RB
    partial = shape((stations, 2 * NBIN), F32)
    edges = [shape((RAMH - 1, half, 2 * NBIN), F32), shape((RAMH, half, 2 * NBIN), F32)]
    middle, ahead, behind, window, last, first = call(
        middle_kernel,
        (shape((stations, inner), BF16), partial, partial, shape((stations, blocks), F32), *edges),
        (raw, sums, table, taper),
        scratch_shapes=[pltpu.VMEM((stations, inner), BF16), pltpu.VMEM((RAMH, half, RB), BF16)],
        flops=4 * stations * inner * NBIN,
    )
    even, odd, factor = call(
        functools.partial(send_kernel, slabs),
        (sent, sent, shape((stations, blocks), F32)),
        (window, even, odd, ahead, behind, last, first),
        flops=4 * stations * RAMH * NBIN,
    )
    even, odd = neighbour_swap(even, odd, False)
    own, keep_right, keep_left = call(
        own_kernel,
        (shape((2 * SUB, NBIN), BF16), kept, kept),
        (raw, factor, middle, table, tapered, taper, ahead, behind, group, nearby, scale),
        scratch_shapes=[
            pltpu.VMEM((stations, samples), BF16),
            pltpu.VMEM((half, RAMH * RB), BF16),
            pltpu.VMEM((half, (RAMH - 1) * RB), BF16),
        ],
        flops=6 * stations * samples * NBIN,
    )
    direct = slabs <= 8 and slabs & (slabs - 1) == 0 and NBIN // slabs % 128 == 0
    width = NBIN // slabs
    rows = 6 * SUB
    pieces = call(
        crossing_kernel,
        tuple([shape((rows, width), BF16)] * slabs) if direct else (shape((rows, NBIN), BF16),),
        (keep_right, keep_left, even, odd, own, group, nearby, scale),
        scratch_shapes=[pltpu.VMEM((rows, NBIN), BF16)],
        flops=8 * stations * NBIN * NBIN,
        limit=32,
    )
    if direct:
        order = far_first(slabs)[1:]
        received = {m: swapped(pieces[m], "tchunk", m) for m in order}
        received = [pieces[0]] + [received[m] for m in far_first(slabs)[1:]]
    else:
        received = pieces[0].reshape(rows, slabs, width).swapaxes(0, 1)
        received = [lax.all_to_all(received, "tchunk", split_axis=0, concat_axis=0, tiled=True)]
    segments = SEG_DEV * slabs - 1
    mine = call(
        functools.partial(combine_kernel, segments, slabs),
        shape((segments * 2 * SUB, width), BF16),
        received,
        scratch_shapes=[pltpu.VMEM((slabs, rows, width), F32)],
    )
    result = (MAXP, width, 2 * SUB * SUB)
    floats = [pltpu.VMEM(mine.shape, F32)] * 2
    flops = segments * width * SUB * SUB * 8
    if count_blocks == 4:
        across = swapped(mine, "stn", 2)
        beside = swapped(mine, "stn", 1)
        last = swapped(across, "stn", 1)
        products = call(
            functools.partial(near_kernel, segments),
            shape(result, F32),
            (mine, beside, across),
            scratch_shapes=floats,
            flops=2 * flops,
        )
        out = call(
            functools.partial(last_kernel, segments),
            shape(result, F32),
            (partner_blocks, mine, last, products),
            out_specs=HBM,
            scratch_shapes=floats + [pltpu.VMEM(result[1:], F32), pltpu.SemaphoreType.DMA((MAXP,))],
            flops=flops,
        )
    else:
        gathered = lax.all_gather(mine, "stn", axis=0)
        others = [lax.dynamic_index_in_dim(gathered, home ^ m, 0, keepdims=False) for m in range(count_blocks)]
        out = call(
            functools.partial(cross_kernel, segments),
            shape(result, F32),
            (partner_blocks, *others),
            out_specs=HBM,
            scratch_shapes=floats + [pltpu.VMEM(result, F32), pltpu.SemaphoreType.DMA((MAXP,))],
            flops=MAXP * flops,
            limit=32,
        )
    return out[None]


def solution(mesh):
    placed = (P("stn", ("hour", "tchunk")), P("stn"), P("stn", None))
    return jax.shard_map(
        body,
        mesh=mesh,
        in_specs=placed,
        out_specs=P(("hour", "stn"), None, "tchunk", None),
        check_vma=False,
    )
```

```python
import functools
import math

import jax
import jax.numpy as jnp
import ml_dtypes
import numpy as np
from jax import lax
from jax.experimental import pallas as pl
from jax.experimental.pallas import tpu as pltpu
from jax.sharding import PartitionSpec as P

SEG_DEV = 2
SEGLEN = 4096
HOP = 2048
NBIN = 512
RB = 128
RAMH = 10
SMOOTH = 8
SUB = 16
MAXP = 3

EPS_MEAN = 1e-06
LEVEL = 0.05

BF16 = jnp.bfloat16
F32 = jnp.float32
VMEM = pl.BlockSpec(memory_space=pltpu.VMEM)
HBM = pl.BlockSpec(memory_space=pltpu.HBM)
MIB = 1 << 20


def dft_tables():
    sample = np.arange(HOP, dtype=np.int32)
    frequency = np.arange(1, NBIN + 1, dtype=np.int32)
    turn = np.arange(SEGLEN, dtype=np.float64) * (2.0 * math.pi / SEGLEN)
    phases = sample[:, None] * frequency[None, :] % SEGLEN
    matrix = np.concatenate([np.cos(turn)[phases], -np.sin(turn)[phases]], axis=1)
    taper = (0.5 - 0.5 * np.cos(turn)).reshape(2, HOP)
    repeated = np.concatenate([matrix, matrix * np.concatenate([(-1.0) ** frequency] * 2)], axis=0)
    tapered = (taper.reshape(-1, 1) * repeated).astype(np.float32).astype(ml_dtypes.bfloat16)
    matrix = matrix.astype(np.float32).astype(ml_dtypes.bfloat16)
    return tapered, matrix, taper.astype(np.float32)


def smooth_tables():
    bin_index = np.arange(NBIN)
    nearby = np.abs(bin_index[:, None] - bin_index[None, :]) <= SMOOTH
    scale = 1.0 / np.sum(nearby, axis=0, keepdims=True)
    return nearby.astype(ml_dtypes.bfloat16), scale.astype(np.float32)


def neighbour_swap(first, second, outer_first):
    blocks, slabs = lax.axis_size("stn"), lax.axis_size("tchunk")
    inner = [(i, i ^ 1) for i in range(slabs - slabs % 2)]
    outer = [(i, i + 1) for i in range(1, slabs - 1, 2)]
    outer += [(j, i) for i, j in outer]
    pairs = [[(b * slabs + i, b * slabs + j) for b in range(blocks) for i, j in part] for part in (inner, outer)]
    if blocks % 2 == 0 and slabs % 2 == 0:
        pairs[1] += [(b * slabs + i, (b ^ 1) * slabs + i) for b in range(blocks) for i in (0, slabs - 1)]
    sent = {}
    for i in (1, 0) if outer_first else (0, 1):
        sent[i] = lax.ppermute((first, second)[i], ("stn", "tchunk"), pairs[i])
    return sent[0], sent[1]


def swapped(block, axis, mask):
    return lax.ppermute(block, axis, [(i, i ^ mask) for i in range(lax.axis_size(axis))])


def call(kernel, out_shape, operands, specs=None, flops=0, limit=16, **more):
    moved = sum(math.prod(a.shape) * a.dtype.itemsize for a in list(operands) + jax.tree.leaves(out_shape))
    more.setdefault("out_specs", jax.tree.map(lambda _: VMEM, out_shape))
    return pl.pallas_call(
        kernel,
        out_shape=out_shape,
        in_specs=specs or [VMEM] * len(operands),
        compiler_params=pltpu.CompilerParams(vmem_limit_bytes=limit * MIB),
        cost_estimate=pl.CostEstimate(flops=flops, bytes_accessed=moved, transcendentals=0),
        **more,
    )(*operands)


def sums_kernel(source, taper_source, raw, sums, to_even, to_odd, taper, held, arrived):
    chunks = arrived.shape[0] - 1
    stations, samples = raw.shape
    blocks = samples // RB
    ends = [stations * n // 9 // 8 * 8 for n in (0, 3, 6, 9)]
    copies = []
    for step in range(chunks):
        rows = ends[step + 1] - ends[step]
        here = pl.ds(ends[step], rows)
        copies.append(pltpu.make_async_copy(source.at[here], raw.at[here], arrived.at[step]))
        copies[-1].start()
    copies.append(pltpu.make_async_copy(taper_source, taper, arrived.at[chunks]))
    copies[-1].start()
    for step in range(chunks):
        copies[step].wait()
        rows = ends[step + 1] - ends[step]
        here = pl.ds(ends[step], rows)
        lane = lax.broadcasted_iota(jnp.int32, (rows, RB), 1)
        total = jnp.zeros((rows, RB), F32)
        for b in range(blocks):
            amount = jnp.sum(jnp.abs(raw[here, b * RB : (b + 1) * RB]), axis=1, keepdims=True)
            total = jnp.where(lane == b, amount, total)
        held[here, :] = total
    whole = held[...]
    sums[...] = whole[:, :blocks]
    flipped = jnp.transpose(whole)
    head = flipped[: blocks // 2]
    tail = flipped[blocks // 2 : blocks]
    even = lax.axis_index("tchunk") % 2 == 0
    to_even[...] = jnp.where(even, tail, head)
    to_odd[...] = jnp.where(even, head, tail)
    copies[-1].wait()


def split_dot(left, right, axis):
    high = left.astype(BF16)
    rest = left - high.astype(F32)
    middle = rest.astype(BF16)
    low = (rest - middle.astype(F32)).astype(BF16)
    parts = jnp.concatenate([high, middle, low], axis=axis)
    return lax.dot_general(
        parts, jnp.concatenate([right] * 3, axis=0), (((axis,), (0,)), ((), ())), preferred_element_type=F32
    )


def band(rows, blocks, first):
    source = lax.broadcasted_iota(jnp.int32, (rows, blocks), 0) + first
    target = lax.broadcasted_iota(jnp.int32, (rows, blocks), 1)
    return ((source >= target - RAMH) & (source < target + RAMH)).astype(BF16)


def alternating():
    column = lax.broadcasted_iota(jnp.int32, (1, 2 * NBIN), 1)
    return jnp.where(column % 2 == 0, -1.0, 1.0)


def windowed_blocks(raw, factor, taper, rows, some, normal, windowed):
    for place, b in enumerate(some):
        here = pl.ds(place * RB, RB)
        scaled = (raw[rows, b * RB : (b + 1) * RB] * factor[rows, b : b + 1]).astype(BF16)
        if normal is not None:
            normal[:, here] = scaled
        hop, inside = divmod(b * RB, HOP)
        weight = taper[1 - hop : 2 - hop, inside : inside + RB]
        windowed[:, here] = (scaled.astype(F32) * weight).astype(BF16)


def middle_kernel(raw, sums, table, taper, normal, ahead, behind, window, last, first, windowed, bare):
    blocks = sums.shape[1]
    half = raw.shape[0] // 2
    for source, rows, some, out in (
        (raw, slice(half, None), range(blocks - RAMH + 1, blocks), last),
        (raw, slice(0, half), range(RAMH), first),
    ):
        for place, b in enumerate(some):
            hop, inside = divmod(b * RB, HOP)
            weight = taper[1 - hop : 2 - hop, inside : inside + RB]
            bare[place] = (source[rows, b * RB : (b + 1) * RB] * weight).astype(BF16)
            out[place] = jnp.dot(bare[place], table[inside : inside + RB, :], preferred_element_type=F32)

    window[...] = split_dot(sums[...], band(blocks, blocks, 0), 1)
    factor = 1.0 / (window[...] * (1.0 / (2 * RAMH * RB)) + EPS_MEAN)
    windowed_blocks(raw, factor, taper, slice(None), range(RAMH, blocks - RAMH + 1), normal, windowed)
    split = HOP - RAMH * RB
    rest = windowed.shape[1] - split
    ahead[...] = jnp.dot(windowed[:, split:], table[:rest, :], preferred_element_type=F32)
    behind[...] = jnp.dot(windowed[:, :split], table[HOP - split :, :], preferred_element_type=F32)


def send_kernel(slabs, window, from_even, from_odd, ahead, behind, last, first, to_even, to_odd, factor):
    stations, blocks = window.shape
    half_blocks = from_even.shape[0]
    half = stations // 2
    me = lax.axis_index("tchunk")
    even = me % 2 == 0
    left = jnp.where(even, from_odd[...], from_even[...])
    right = jnp.where(even, from_even[...], from_odd[...])
    left = jnp.where(me > 0, left, 0.0)
    right = jnp.where(me < slabs - 1, right, 0.0)
    near = jnp.concatenate([left, right], axis=0)
    bands = jnp.concatenate([band(half_blocks, blocks, -half_blocks), band(half_blocks, blocks, blocks)], axis=0)
    total = window[...] + split_dot(near, bands, 0)
    block = lax.broadcasted_iota(jnp.int32, (stations, blocks), 1) + me * blocks
    counted = jnp.minimum(block + RAMH, slabs * blocks) - jnp.maximum(block - RAMH, 0)
    factor[...] = 1.0 / (total / (RB * counted.astype(F32)) + EPS_MEAN)
    sign = alternating()

    def weighted(base, products, start, first):
        sums = []
        for row in range(0, half, 8):
            here = slice(start + row, start + row + 8)
            total = base[here, :]
            for place in range(products.shape[0]):
                b = first + place
                total += factor[here, b : b + 1] * products[place, row : row + 8, :]
            sums.append(total)
        return jnp.concatenate(sums, axis=0)

    def fill(to_right, to_left):
        to_right[...] = weighted(ahead, last, half, blocks - RAMH + 1).astype(BF16)
        to_left[...] = (weighted(behind, first, 0, 0) * sign).astype(BF16)

    @pl.when(even)
    def _():
        fill(to_even, to_odd)

    @pl.when(jnp.logical_not(even))
    def _():
        fill(to_odd, to_even)


def whiten(spectra, nearby, scale):
    rows = spectra.shape[0]
    real_part = spectra[:, :NBIN]
    imag_part = spectra[:, NBIN:]
    powers = real_part * real_part + imag_part * imag_part
    high = powers.astype(BF16)
    low = (powers - high.astype(F32)).astype(BF16)
    both = jnp.dot(jnp.concatenate([high, low], axis=0), nearby, preferred_element_type=F32)
    smooth = both[:rows] + both[rows:]
    floor_level = jnp.sum(powers, axis=1, keepdims=True) * (1.0 / NBIN) + 1e-06
    inverse = lax.rsqrt(smooth * scale + LEVEL * floor_level)
    return (real_part * inverse).astype(BF16), (imag_part * inverse).astype(BF16)


def members(group, count):
    shape = (count, group.shape[1])
    return (lax.broadcasted_iota(jnp.int32, shape, 0) == group).astype(BF16)


def own_kernel(
    raw, factor, middle, table, tapered, taper, ahead, behind, group, nearby, scale,
    beams, keep_right, keep_left, normal, first, last,
):
    stations, blocks = factor.shape
    half = stations // 2
    windowed_blocks(raw, factor, taper, slice(0, half), range(blocks - RAMH + 1, blocks), None, last)
    windowed_blocks(raw, factor, taper, slice(half, stations), range(RAMH), None, first)
    part = jnp.dot(last[...], table[HOP - last.shape[1] :, :], preferred_element_type=F32)
    keep_right[...] = part + ahead[:half]
    part = jnp.dot(first[...], table[: first.shape[1], :], preferred_element_type=F32)
    keep_left[...] = (part + behind[half:]) * alternating()

    for b in [*range(RAMH), *range(blocks - RAMH + 1, blocks)]:
        here = pl.ds(b * RB, RB)
        normal[:, here] = (raw[:, here] * factor[:, b : b + 1]).astype(BF16)
    normal[:, RAMH * RB : RAMH * RB + middle.shape[1]] = middle[...]
    spectra = jnp.dot(normal[...], tapered[...], preferred_element_type=F32)
    member = members(group[...], SUB)
    for part, white in enumerate(whiten(spectra, nearby[...], scale[...])):
        beams[part * SUB : (part + 1) * SUB, :] = jnp.dot(member, white, preferred_element_type=F32).astype(BF16)


def crossing_kernel(keep_right, keep_left, from_even, from_odd, own, group, nearby, scale, *out):
    half = keep_right.shape[0]
    held = out[-1]
    me = lax.axis_index("tchunk")
    even = me % 2 == 0
    got_even, got_odd = from_even[...], from_odd[...]
    ahead = keep_right[...] + jnp.where(even, got_even, got_odd).astype(F32)
    behind = keep_left[...] + jnp.where(even, got_odd, got_even).astype(F32)
    spectra = jnp.concatenate([ahead, behind], axis=0)
    station = lax.broadcasted_iota(jnp.int32, group.shape, 1)
    member = members(group[...] + jnp.where(station < half, 0, SUB), 2 * SUB)
    held[: 2 * SUB, :] = own[...]
    for part, white in enumerate(whiten(spectra, nearby[...], scale[...])):
        sums = jnp.dot(member, white, preferred_element_type=F32).astype(BF16)
        for side in range(2):
            row = (2 + 2 * side + part) * SUB
            held[row : row + SUB, :] = sums[side * SUB : (side + 1) * SUB]
    pieces = len(out) - 1
    if pieces > 1:
        width = NBIN // pieces
        for mask in range(pieces):
            start = pl.multiple_of((me ^ mask) * width, width)
            out[mask][...] = held[:, pl.ds(start, width)]
    else:
        out[0][...] = held[...]


def far_first(slabs):
    return [0, *range(slabs - 1, 0, -1)]


def combine_kernel(segments, slabs, *refs):
    pieces, (out, held) = refs[:-2], refs[-2:]
    me = lax.axis_index("tchunk")
    side = 2 * SUB
    order = far_first(slabs)
    for m in range(slabs):
        if len(pieces) == slabs:
            held[me ^ order[m]] = pieces[m][...].astype(F32)
        else:
            held[m] = pieces[0][m].astype(F32)
    for s in range(segments):
        here = held[s // 2, :side, :]
        if s % 2 == 1:
            here = held[s // 2, side : 2 * side, :] + held[s // 2 + 1, 2 * side :, :]
        out[s * side : (s + 1) * side, :] = here.astype(BF16)


def cross_terms(segments, mine, others, out):
    side = 2 * SUB
    real, imag = [], []
    for q in range(SUB):
        real_sum = jnp.zeros((SUB, mine.shape[1]), F32)
        imag_sum = jnp.zeros((SUB, mine.shape[1]), F32)
        for s in range(segments):
            first = s * side
            a, b = mine[first + q : first + q + 1, :], mine[first + SUB + q : first + SUB + q + 1, :]
            c, d = others[first : first + SUB, :], others[first + SUB : first + side, :]
            real_sum += a * c + b * d
            imag_sum += b * c - a * d
        real.append(real_sum * (1.0 / segments))
        imag.append(imag_sum * (1.0 / segments))
    half = SUB * SUB
    out[:, :half] = jnp.transpose(jnp.concatenate(real, axis=0))
    out[:, half:] = jnp.transpose(jnp.concatenate(imag, axis=0))


def near_kernel(segments, own, *refs):
    blocks, (products, mine, others) = refs[:-3], refs[-3:]
    mine[...] = own[...].astype(F32)
    products[0] = jnp.zeros(products.shape[1:], F32)
    for index, block in enumerate(blocks):
        others[...] = block[...].astype(F32)
        cross_terms(segments, mine, others, products.at[index + 1])


def last_kernel(segments, partners, own, block, products, out, mine, others, last, finished):
    home = lax.axis_index("stn")
    count = products.shape[0]
    which = []
    for slot in range(MAXP):
        partner = jnp.max(partners[0:1, slot : slot + 1])
        which.append(jnp.where(partner < 0, 0, partner ^ home))

    def copy(slot, source):
        return pltpu.make_async_copy(source, out.at[slot], finished.at[slot])

    for slot in range(MAXP):
        @pl.when(which[slot] < count)
        def _(slot=slot):
            copy(slot, products.at[jnp.where(which[slot] == 0, 0, 3 - jnp.minimum(which[slot], count - 1))]).start()

    mine[...] = own[...].astype(F32)
    others[...] = block[...].astype(F32)
    cross_terms(segments, mine, others, last)
    for slot in range(MAXP):
        @pl.when(which[slot] >= count)
        def _(slot=slot):
            copy(slot, last).start()

    for slot in range(MAXP):
        copy(slot, last).wait()


def cross_kernel(segments, partners, *refs):
    blocks, (out, mine, others, done, finished) = refs[:-5], refs[-5:]
    home = lax.axis_index("stn")
    mine[...] = blocks[0][...].astype(F32)
    copies = []
    for slot in range(MAXP):
        partner = partners[0:1, slot : slot + 1]
        chosen = jnp.zeros(mine.shape, F32)
        for index in range(1, len(blocks)):
            chosen = jnp.where(partner == home ^ index, blocks[index][...].astype(F32), chosen)
        others[...] = chosen
        cross_terms(segments, mine, others, done.at[slot])
        copies.append(pltpu.make_async_copy(done.at[slot], out.at[slot], finished.at[slot]))
        copies[-1].start()
    for copy in copies:
        copy.wait()


def body(raw_data, station_group, partner_blocks):
    stations, samples = raw_data.shape
    slabs = lax.axis_size("tchunk")
    count_blocks = lax.axis_size("stn")
    me, home = lax.axis_index("tchunk"), lax.axis_index("stn")
    blocks = samples // RB
    half = stations // 2
    tapered, table, taper = (jnp.asarray(t) for t in dft_tables())
    nearby, scale = (jnp.asarray(t) for t in smooth_tables())
    group = station_group[None, :]
    shape = jax.ShapeDtypeStruct

    halo = shape((blocks // 2, stations), F32)
    in_hbm = [pltpu.with_memory_space_constraint(a, pltpu.HBM) for a in (raw_data, taper, table)]
    raw, sums, even, odd, taper = call(
        sums_kernel,
        (shape(raw_data.shape, F32), shape((stations, blocks), F32), halo, halo, shape(taper.shape, F32)),
        in_hbm[:2],
        specs=[HBM, HBM],
        scratch_shapes=[pltpu.VMEM((stations, RB), F32), pltpu.SemaphoreType.DMA((4,))],
        flops=10**10,
    )
    even, odd = neighbour_swap(even, odd, True)
    sent = shape((half, 2 * NBIN), BF16)
    kept = shape((half, 2 * NBIN), F32)
    inner = (blocks - 2 * RAMH + 1) * RB
    partial = shape((stations, 2 * NBIN), F32)
    edges = [shape((RAMH - 1, half, 2 * NBIN), F32), shape((RAMH, half, 2 * NBIN), F32)]
    middle, ahead, behind, window, last, first = call(
        middle_kernel,
        (shape((stations, inner), BF16), partial, partial, shape((stations, blocks), F32), *edges),
        (raw, sums, table, taper),
        scratch_shapes=[pltpu.VMEM((stations, inner), BF16), pltpu.VMEM((RAMH, half, RB), BF16)],
        flops=4 * stations * inner * NBIN,
    )
    even, odd, factor = call(
        functools.partial(send_kernel, slabs),
        (sent, sent, shape((stations, blocks), F32)),
        (window, even, odd, ahead, behind, last, first),
        flops=4 * stations * RAMH * NBIN,
    )
    even, odd = neighbour_swap(even, odd, False)
    own, keep_right, keep_left = call(
        own_kernel,
        (shape((2 * SUB, NBIN), BF16), kept, kept),
        (raw, factor, middle, table, tapered, taper, ahead, behind, group, nearby, scale),
        scratch_shapes=[
            pltpu.VMEM((stations, samples), BF16),
            pltpu.VMEM((half, RAMH * RB), BF16),
            pltpu.VMEM((half, (RAMH - 1) * RB), BF16),
        ],
        flops=6 * stations * samples * NBIN,
    )
    direct = slabs <= 8 and slabs & (slabs - 1) == 0 and NBIN // slabs % 128 == 0
    width = NBIN // slabs
    rows = 6 * SUB
    pieces = call(
        crossing_kernel,
        tuple([shape((rows, width), BF16)] * slabs) if direct else (shape((rows, NBIN), BF16),),
        (keep_right, keep_left, even, odd, own, group, nearby, scale),
        scratch_shapes=[pltpu.VMEM((rows, NBIN), BF16)],
        flops=8 * stations * NBIN * NBIN,
        limit=32,
    )
    if direct:
        order = far_first(slabs)[1:]
        received = {m: swapped(pieces[m], "tchunk", m) for m in order}
        received = [pieces[0]] + [received[m] for m in far_first(slabs)[1:]]
    else:
        received = pieces[0].reshape(rows, slabs, width).swapaxes(0, 1)
        received = [lax.all_to_all(received, "tchunk", split_axis=0, concat_axis=0, tiled=True)]
    segments = SEG_DEV * slabs - 1
    mine = call(
        functools.partial(combine_kernel, segments, slabs),
        shape((segments * 2 * SUB, width), BF16),
        received,
        scratch_shapes=[pltpu.VMEM((slabs, rows, width), F32)],
    )
    result = (MAXP, width, 2 * SUB * SUB)
    floats = [pltpu.VMEM(mine.shape, F32)] * 2
    flops = segments * width * SUB * SUB * 8
    if count_blocks == 4:
        across = swapped(mine, "stn", 2)
        beside = swapped(mine, "stn", 1)
        last = swapped(across, "stn", 1)
        products = call(
            functools.partial(near_kernel, segments),
            shape(result, F32),
            (mine, across, beside),
            scratch_shapes=floats,
            flops=2 * flops,
        )
        out = call(
            functools.partial(last_kernel, segments),
            shape(result, F32),
            (partner_blocks, mine, last, products),
            out_specs=HBM,
            scratch_shapes=floats + [pltpu.VMEM(result[1:], F32), pltpu.SemaphoreType.DMA((MAXP,))],
            flops=flops,
        )
    else:
        gathered = lax.all_gather(mine, "stn", axis=0)
        others = [lax.dynamic_index_in_dim(gathered, home ^ m, 0, keepdims=False) for m in range(count_blocks)]
        out = call(
            functools.partial(cross_kernel, segments),
            shape(result, F32),
            (partner_blocks, *others),
            out_specs=HBM,
            scratch_shapes=floats + [pltpu.VMEM(result, F32), pltpu.SemaphoreType.DMA((MAXP,))],
            flops=MAXP * flops,
            limit=32,
        )
    return out[None]


def solution(mesh):
    placed = (P("stn", ("hour", "tchunk")), P("stn"), P("stn", None))
    return jax.shard_map(
        body,
        mesh=mesh,
        in_specs=placed,
        out_specs=P(("hour", "stn"), None, "tchunk", None),
        check_vma=False,
    )
```

```python
import functools
import math

import jax
import jax.numpy as jnp
import ml_dtypes
import numpy as np
from jax import lax
from jax.experimental import pallas as pl
from jax.experimental.pallas import tpu as pltpu
from jax.sharding import PartitionSpec as P

SEG_DEV = 2
SEGLEN = 4096
HOP = 2048
NBIN = 512
RB = 128
RAMH = 10
SMOOTH = 8
SUB = 16
MAXP = 3

EPS_MEAN = 1e-06
LEVEL = 0.05

BF16 = jnp.bfloat16
F32 = jnp.float32
VMEM = pl.BlockSpec(memory_space=pltpu.VMEM)
HBM = pl.BlockSpec(memory_space=pltpu.HBM)
MIB = 1 << 20


def dft_tables():
    sample = np.arange(HOP, dtype=np.int32)
    frequency = np.arange(1, NBIN + 1, dtype=np.int32)
    turn = np.arange(SEGLEN, dtype=np.float64) * (2.0 * math.pi / SEGLEN)
    phases = sample[:, None] * frequency[None, :] % SEGLEN
    matrix = np.concatenate([np.cos(turn)[phases], -np.sin(turn)[phases]], axis=1)
    taper = (0.5 - 0.5 * np.cos(turn)).reshape(2, HOP)
    repeated = np.concatenate([matrix, matrix * np.concatenate([(-1.0) ** frequency] * 2)], axis=0)
    tapered = (taper.reshape(-1, 1) * repeated).astype(np.float32).astype(ml_dtypes.bfloat16)
    matrix = matrix.astype(np.float32).astype(ml_dtypes.bfloat16)
    return tapered, matrix, taper.astype(np.float32)


def smooth_tables():
    bin_index = np.arange(NBIN)
    nearby = np.abs(bin_index[:, None] - bin_index[None, :]) <= SMOOTH
    scale = 1.0 / np.sum(nearby, axis=0, keepdims=True)
    return nearby.astype(ml_dtypes.bfloat16), scale.astype(np.float32)


def neighbour_swap(first, second, outer_first):
    blocks, slabs = lax.axis_size("stn"), lax.axis_size("tchunk")
    inner = [(i, i ^ 1) for i in range(slabs - slabs % 2)]
    outer = [(i, i + 1) for i in range(1, slabs - 1, 2)]
    outer += [(j, i) for i, j in outer]
    pairs = [[(b * slabs + i, b * slabs + j) for b in range(blocks) for i, j in part] for part in (inner, outer)]
    if blocks % 2 == 0 and slabs % 2 == 0:
        pairs[1] += [(b * slabs + i, (b ^ 1) * slabs + i) for b in range(blocks) for i in (0, slabs - 1)]
    sent = {}
    for i in (1, 0) if outer_first else (0, 1):
        sent[i] = lax.ppermute((first, second)[i], ("stn", "tchunk"), pairs[i])
    return sent[0], sent[1]


def swapped(block, axis, mask):
    return lax.ppermute(block, axis, [(i, i ^ mask) for i in range(lax.axis_size(axis))])


def call(kernel, out_shape, operands, specs=None, flops=0, limit=16, **more):
    moved = sum(math.prod(a.shape) * a.dtype.itemsize for a in list(operands) + jax.tree.leaves(out_shape))
    more.setdefault("out_specs", jax.tree.map(lambda _: VMEM, out_shape))
    return pl.pallas_call(
        kernel,
        out_shape=out_shape,
        in_specs=specs or [VMEM] * len(operands),
        compiler_params=pltpu.CompilerParams(vmem_limit_bytes=limit * MIB),
        cost_estimate=pl.CostEstimate(flops=flops, bytes_accessed=moved, transcendentals=0),
        **more,
    )(*operands)


def sums_kernel(source, taper_source, raw, sums, to_even, to_odd, taper, held, arrived):
    chunks = arrived.shape[0] - 1
    stations, samples = raw.shape
    blocks = samples // RB
    ends = [stations * n // 9 // 8 * 8 for n in (0, 3, 6, 9)]
    copies = []
    for step in range(chunks):
        rows = ends[step + 1] - ends[step]
        here = pl.ds(ends[step], rows)
        copies.append(pltpu.make_async_copy(source.at[here], raw.at[here], arrived.at[step]))
        copies[-1].start()
    copies.append(pltpu.make_async_copy(taper_source, taper, arrived.at[chunks]))
    copies[-1].start()
    for step in range(chunks):
        copies[step].wait()
        rows = ends[step + 1] - ends[step]
        here = pl.ds(ends[step], rows)
        lane = lax.broadcasted_iota(jnp.int32, (rows, RB), 1)
        total = jnp.zeros((rows, RB), F32)
        for b in range(blocks):
            amount = jnp.sum(jnp.abs(raw[here, b * RB : (b + 1) * RB]), axis=1, keepdims=True)
            total = jnp.where(lane == b, amount, total)
        held[here, :] = total
    whole = held[...]
    sums[...] = whole[:, :blocks]
    flipped = jnp.transpose(whole)
    head = flipped[: blocks // 2]
    tail = flipped[blocks // 2 : blocks]
    even = lax.axis_index("tchunk") % 2 == 0
    to_even[...] = jnp.where(even, tail, head)
    to_odd[...] = jnp.where(even, head, tail)
    copies[-1].wait()


def split_dot(left, right, axis):
    high = left.astype(BF16)
    rest = left - high.astype(F32)
    middle = rest.astype(BF16)
    low = (rest - middle.astype(F32)).astype(BF16)
    parts = jnp.concatenate([high, middle, low], axis=axis)
    return lax.dot_general(
        parts, jnp.concatenate([right] * 3, axis=0), (((axis,), (0,)), ((), ())), preferred_element_type=F32
    )


def band(rows, blocks, first):
    source = lax.broadcasted_iota(jnp.int32, (rows, blocks), 0) + first
    target = lax.broadcasted_iota(jnp.int32, (rows, blocks), 1)
    return ((source >= target - RAMH) & (source < target + RAMH)).astype(BF16)


def alternating():
    column = lax.broadcasted_iota(jnp.int32, (1, 2 * NBIN), 1)
    return jnp.where(column % 2 == 0, -1.0, 1.0)


def windowed_blocks(raw, factor, taper, rows, some, normal, windowed):
    for place, b in enumerate(some):
        here = pl.ds(place * RB, RB)
        scaled = (raw[rows, b * RB : (b + 1) * RB] * factor[rows, b : b + 1]).astype(BF16)
        if normal is not None:
            normal[:, here] = scaled
        hop, inside = divmod(b * RB, HOP)
        weight = taper[1 - hop : 2 - hop, inside : inside + RB]
        windowed[:, here] = (scaled.astype(F32) * weight).astype(BF16)


def middle_kernel(raw, sums, table, taper, normal, ahead, behind, window, last, first, windowed, bare):
    blocks = sums.shape[1]
    half = raw.shape[0] // 2
    for source, rows, some, out in (
        (raw, slice(half, None), range(blocks - RAMH + 1, blocks), last),
        (raw, slice(0, half), range(RAMH), first),
    ):
        for place, b in enumerate(some):
            hop, inside = divmod(b * RB, HOP)
            weight = taper[1 - hop : 2 - hop, inside : inside + RB]
            bare[place] = (source[rows, b * RB : (b + 1) * RB] * weight).astype(BF16)
            out[place] = jnp.dot(bare[place], table[inside : inside + RB, :], preferred_element_type=F32)

    window[...] = split_dot(sums[...], band(blocks, blocks, 0), 1)
    factor = 1.0 / (window[...] * (1.0 / (2 * RAMH * RB)) + EPS_MEAN)
    windowed_blocks(raw, factor, taper, slice(None), range(RAMH, blocks - RAMH + 1), normal, windowed)
    split = HOP - RAMH * RB
    rest = windowed.shape[1] - split
    ahead[...] = jnp.dot(windowed[:, split:], table[:rest, :], preferred_element_type=F32)
    behind[...] = jnp.dot(windowed[:, :split], table[HOP - split :, :], preferred_element_type=F32)


def send_kernel(slabs, window, from_even, from_odd, ahead, behind, last, first, to_even, to_odd, factor):
    stations, blocks = window.shape
    half_blocks = from_even.shape[0]
    half = stations // 2
    me = lax.axis_index("tchunk")
    even = me % 2 == 0
    left = jnp.where(even, from_odd[...], from_even[...])
    right = jnp.where(even, from_even[...], from_odd[...])
    left = jnp.where(me > 0, left, 0.0)
    right = jnp.where(me < slabs - 1, right, 0.0)
    near = jnp.concatenate([left, right], axis=0)
    bands = jnp.concatenate([band(half_blocks, blocks, -half_blocks), band(half_blocks, blocks, blocks)], axis=0)
    total = window[...] + split_dot(near, bands, 0)
    block = lax.broadcasted_iota(jnp.int32, (stations, blocks), 1) + me * blocks
    counted = jnp.minimum(block + RAMH, slabs * blocks) - jnp.maximum(block - RAMH, 0)
    factor[...] = 1.0 / (total / (RB * counted.astype(F32)) + EPS_MEAN)
    sign = alternating()

    def weighted(base, products, start, first):
        sums = []
        for row in range(0, half, 8):
            here = slice(start + row, start + row + 8)
            total = base[here, :]
            for place in range(products.shape[0]):
                b = first + place
                total += factor[here, b : b + 1] * products[place, row : row + 8, :]
            sums.append(total)
        return jnp.concatenate(sums, axis=0)

    def fill(to_right, to_left):
        to_right[...] = weighted(ahead, last, half, blocks - RAMH + 1).astype(BF16)
        to_left[...] = (weighted(behind, first, 0, 0) * sign).astype(BF16)

    @pl.when(even)
    def _():
        fill(to_even, to_odd)

    @pl.when(jnp.logical_not(even))
    def _():
        fill(to_odd, to_even)


def whiten(spectra, nearby, scale):
    rows = spectra.shape[0]
    real_part = spectra[:, :NBIN]
    imag_part = spectra[:, NBIN:]
    powers = real_part * real_part + imag_part * imag_part
    high = powers.astype(BF16)
    low = (powers - high.astype(F32)).astype(BF16)
    both = jnp.dot(jnp.concatenate([high, low], axis=0), nearby, preferred_element_type=F32)
    smooth = both[:rows] + both[rows:]
    floor_level = jnp.sum(powers, axis=1, keepdims=True) * (1.0 / NBIN) + 1e-06
    inverse = lax.rsqrt(smooth * scale + LEVEL * floor_level)
    return (real_part * inverse).astype(BF16), (imag_part * inverse).astype(BF16)


def members(group, count):
    shape = (count, group.shape[1])
    return (lax.broadcasted_iota(jnp.int32, shape, 0) == group).astype(BF16)


def own_kernel(
    raw, factor, middle, table, tapered, taper, ahead, behind, group, nearby, scale,
    beams, keep_right, keep_left, normal, first, last,
):
    stations, blocks = factor.shape
    half = stations // 2
    windowed_blocks(raw, factor, taper, slice(0, half), range(blocks - RAMH + 1, blocks), None, last)
    windowed_blocks(raw, factor, taper, slice(half, stations), range(RAMH), None, first)
    part = jnp.dot(last[...], table[HOP - last.shape[1] :, :], preferred_element_type=F32)
    keep_right[...] = part + ahead[:half]
    part = jnp.dot(first[...], table[: first.shape[1], :], preferred_element_type=F32)
    keep_left[...] = (part + behind[half:]) * alternating()

    for b in [*range(RAMH), *range(blocks - RAMH + 1, blocks)]:
        here = pl.ds(b * RB, RB)
        normal[:, here] = (raw[:, here] * factor[:, b : b + 1]).astype(BF16)
    normal[:, RAMH * RB : RAMH * RB + middle.shape[1]] = middle[...]
    spectra = jnp.dot(normal[...], tapered[...], preferred_element_type=F32)
    member = members(group[...], SUB)
    for part, white in enumerate(whiten(spectra, nearby[...], scale[...])):
        beams[part * SUB : (part + 1) * SUB, :] = jnp.dot(member, white, preferred_element_type=F32).astype(BF16)


def crossing_kernel(keep_right, keep_left, from_even, from_odd, own, group, nearby, scale, *out):
    half = keep_right.shape[0]
    held = out[-1]
    me = lax.axis_index("tchunk")
    even = me % 2 == 0
    got_even, got_odd = from_even[...], from_odd[...]
    ahead = keep_right[...] + jnp.where(even, got_even, got_odd).astype(F32)
    behind = keep_left[...] + jnp.where(even, got_odd, got_even).astype(F32)
    spectra = jnp.concatenate([ahead, behind], axis=0)
    station = lax.broadcasted_iota(jnp.int32, group.shape, 1)
    member = members(group[...] + jnp.where(station < half, 0, SUB), 2 * SUB)
    held[: 2 * SUB, :] = own[...]
    for part, white in enumerate(whiten(spectra, nearby[...], scale[...])):
        sums = jnp.dot(member, white, preferred_element_type=F32).astype(BF16)
        for side in range(2):
            row = (2 + 2 * side + part) * SUB
            held[row : row + SUB, :] = sums[side * SUB : (side + 1) * SUB]
    pieces = len(out) - 1
    if pieces > 1:
        width = NBIN // pieces
        for mask in range(pieces):
            start = pl.multiple_of((me ^ mask) * width, width)
            out[mask][...] = held[:, pl.ds(start, width)]
    else:
        out[0][...] = held[...]


def far_first(slabs):
    return [0, *range(slabs - 1, 0, -1)]


def combine_kernel(segments, slabs, *refs):
    pieces, (out, held) = refs[:-2], refs[-2:]
    me = lax.axis_index("tchunk")
    side = 2 * SUB
    order = far_first(slabs)
    for m in range(slabs):
        if len(pieces) == slabs:
            held[me ^ order[m]] = pieces[m][...].astype(F32)
        else:
            held[m] = pieces[0][m].astype(F32)
    for s in range(segments):
        here = held[s // 2, :side, :]
        if s % 2 == 1:
            here = held[s // 2, side : 2 * side, :] + held[s // 2 + 1, 2 * side :, :]
        out[s * side : (s + 1) * side, :] = here.astype(BF16)


def cross_terms(segments, mine, others, out):
    side = 2 * SUB
    theirs = []
    for s in range(segments):
        c, d = others[s * side : s * side + SUB, :], others[s * side + SUB : (s + 1) * side, :]
        theirs.append((c, c + d, c - d))
    real, imag = [], []
    for q in range(SUB):
        shared = jnp.zeros((SUB, mine.shape[1]), F32)
        first, second = shared, shared
        for s, (c, plus, minus) in enumerate(theirs):
            row = s * side + q
            a, b = mine[row : row + 1, :], mine[row + SUB : row + SUB + 1, :]
            shared += (a + b) * c
            first += b * minus
            second += a * plus
        real.append((shared - first) * (1.0 / segments))
        imag.append((shared - second) * (1.0 / segments))
    half = SUB * SUB
    out[:, :half] = jnp.transpose(jnp.concatenate(real, axis=0))
    out[:, half:] = jnp.transpose(jnp.concatenate(imag, axis=0))


def near_kernel(segments, own, *refs):
    blocks, (products, mine, others) = refs[:-3], refs[-3:]
    mine[...] = own[...].astype(F32)
    products[0] = jnp.zeros(products.shape[1:], F32)
    for index, block in enumerate(blocks):
        others[...] = block[...].astype(F32)
        cross_terms(segments, mine, others, products.at[index + 1])


def last_kernel(segments, partners, own, block, products, out, mine, others, last, finished):
    home = lax.axis_index("stn")
    count = products.shape[0]
    which = []
    for slot in range(MAXP):
        partner = jnp.max(partners[0:1, slot : slot + 1])
        which.append(jnp.where(partner < 0, 0, partner ^ home))

    def copy(slot, source):
        return pltpu.make_async_copy(source, out.at[slot], finished.at[slot])

    for slot in range(MAXP):
        @pl.when(which[slot] < count)
        def _(slot=slot):
            copy(slot, products.at[jnp.minimum(which[slot], count - 1)]).start()

    mine[...] = own[...].astype(F32)
    others[...] = block[...].astype(F32)
    cross_terms(segments, mine, others, last)
    for slot in range(MAXP):
        @pl.when(which[slot] >= count)
        def _(slot=slot):
            copy(slot, last).start()

    for slot in range(MAXP):
        copy(slot, last).wait()


def cross_kernel(segments, partners, *refs):
    blocks, (out, mine, others, done, finished) = refs[:-5], refs[-5:]
    home = lax.axis_index("stn")
    mine[...] = blocks[0][...].astype(F32)
    copies = []
    for slot in range(MAXP):
        partner = partners[0:1, slot : slot + 1]
        chosen = jnp.zeros(mine.shape, F32)
        for index in range(1, len(blocks)):
            chosen = jnp.where(partner == home ^ index, blocks[index][...].astype(F32), chosen)
        others[...] = chosen
        cross_terms(segments, mine, others, done.at[slot])
        copies.append(pltpu.make_async_copy(done.at[slot], out.at[slot], finished.at[slot]))
        copies[-1].start()
    for copy in copies:
        copy.wait()


def body(raw_data, station_group, partner_blocks):
    stations, samples = raw_data.shape
    slabs = lax.axis_size("tchunk")
    count_blocks = lax.axis_size("stn")
    me, home = lax.axis_index("tchunk"), lax.axis_index("stn")
    blocks = samples // RB
    half = stations // 2
    tapered, table, taper = (jnp.asarray(t) for t in dft_tables())
    nearby, scale = (jnp.asarray(t) for t in smooth_tables())
    group = station_group[None, :]
    shape = jax.ShapeDtypeStruct

    halo = shape((blocks // 2, stations), F32)
    in_hbm = [pltpu.with_memory_space_constraint(a, pltpu.HBM) for a in (raw_data, taper, table)]
    raw, sums, even, odd, taper = call(
        sums_kernel,
        (shape(raw_data.shape, F32), shape((stations, blocks), F32), halo, halo, shape(taper.shape, F32)),
        in_hbm[:2],
        specs=[HBM, HBM],
        scratch_shapes=[pltpu.VMEM((stations, RB), F32), pltpu.SemaphoreType.DMA((4,))],
        flops=10**10,
    )
    even, odd = neighbour_swap(even, odd, True)
    sent = shape((half, 2 * NBIN), BF16)
    kept = shape((half, 2 * NBIN), F32)
    inner = (blocks - 2 * RAMH + 1) * RB
    partial = shape((stations, 2 * NBIN), F32)
    edges = [shape((RAMH - 1, half, 2 * NBIN), F32), shape((RAMH, half, 2 * NBIN), F32)]
    middle, ahead, behind, window, last, first = call(
        middle_kernel,
        (shape((stations, inner), BF16), partial, partial, shape((stations, blocks), F32), *edges),
        (raw, sums, table, taper),
        scratch_shapes=[pltpu.VMEM((stations, inner), BF16), pltpu.VMEM((RAMH, half, RB), BF16)],
        flops=4 * stations * inner * NBIN,
    )
    even, odd, factor = call(
        functools.partial(send_kernel, slabs),
        (sent, sent, shape((stations, blocks), F32)),
        (window, even, odd, ahead, behind, last, first),
        flops=4 * stations * RAMH * NBIN,
    )
    even, odd = neighbour_swap(even, odd, False)
    own, keep_right, keep_left = call(
        own_kernel,
        (shape((2 * SUB, NBIN), BF16), kept, kept),
        (raw, factor, middle, table, tapered, taper, ahead, behind, group, nearby, scale),
        scratch_shapes=[
            pltpu.VMEM((stations, samples), BF16),
            pltpu.VMEM((half, RAMH * RB), BF16),
            pltpu.VMEM((half, (RAMH - 1) * RB), BF16),
        ],
        flops=6 * stations * samples * NBIN,
    )
    direct = slabs <= 8 and slabs & (slabs - 1) == 0 and NBIN // slabs % 128 == 0
    width = NBIN // slabs
    rows = 6 * SUB
    pieces = call(
        crossing_kernel,
        tuple([shape((rows, width), BF16)] * slabs) if direct else (shape((rows, NBIN), BF16),),
        (keep_right, keep_left, even, odd, own, group, nearby, scale),
        scratch_shapes=[pltpu.VMEM((rows, NBIN), BF16)],
        flops=8 * stations * NBIN * NBIN,
        limit=32,
    )
    if direct:
        order = far_first(slabs)[1:]
        received = {m: swapped(pieces[m], "tchunk", m) for m in order}
        received = [pieces[0]] + [received[m] for m in far_first(slabs)[1:]]
    else:
        received = pieces[0].reshape(rows, slabs, width).swapaxes(0, 1)
        received = [lax.all_to_all(received, "tchunk", split_axis=0, concat_axis=0, tiled=True)]
    segments = SEG_DEV * slabs - 1
    mine = call(
        functools.partial(combine_kernel, segments, slabs),
        shape((segments * 2 * SUB, width), BF16),
        received,
        scratch_shapes=[pltpu.VMEM((slabs, rows, width), F32)],
    )
    result = (MAXP, width, 2 * SUB * SUB)
    floats = [pltpu.VMEM(mine.shape, F32)] * 2
    flops = segments * width * SUB * SUB * 8
    if count_blocks == 4:
        across = swapped(mine, "stn", 2)
        beside = swapped(mine, "stn", 1)
        last = swapped(across, "stn", 1)
        products = call(
            functools.partial(near_kernel, segments),
            shape(result, F32),
            (mine, beside, across),
            scratch_shapes=floats,
            flops=2 * flops,
        )
        out = call(
            functools.partial(last_kernel, segments),
            shape(result, F32),
            (partner_blocks, mine, last, products),
            out_specs=HBM,
            scratch_shapes=floats + [pltpu.VMEM(result[1:], F32), pltpu.SemaphoreType.DMA((MAXP,))],
            flops=flops,
        )
    else:
        gathered = lax.all_gather(mine, "stn", axis=0)
        others = [lax.dynamic_index_in_dim(gathered, home ^ m, 0, keepdims=False) for m in range(count_blocks)]
        out = call(
            functools.partial(cross_kernel, segments),
            shape(result, F32),
            (partner_blocks, *others),
            out_specs=HBM,
            scratch_shapes=floats + [pltpu.VMEM(result, F32), pltpu.SemaphoreType.DMA((MAXP,))],
            flops=MAXP * flops,
            limit=32,
        )
    return out[None]


def solution(mesh):
    placed = (P("stn", ("hour", "tchunk")), P("stn"), P("stn", None))
    return jax.shard_map(
        body,
        mesh=mesh,
        in_specs=placed,
        out_specs=P(("hour", "stn"), None, "tchunk", None),
        check_vma=False,
    )
```
